256 devices in a mesh: section: 4 (over y), dp: 16 (over z, x_lo), tensor: 4 (over x_hi, core).
Axes of the slice: x: 4 (x_hi: 2, x_lo: 2; x = x_hi * 2 + x_lo), y: 4, z: 8, core: 2. Of those that a mesh axis runs over, the one named last changes fastest.
Arguments:
- hidden_in: bfloat16 [16, 2, 64, 4096], P('dp', None, None, 'tensor'), may hold values from -6 to 6
- teacher: bfloat16 [16, 2, 64, 4096], P('dp', None, None, 'tensor'), may hold values from -6 to 6
- segment_ids: int32 [16, 2, 64], P('dp'), may hold values from 0 to 3, never falling along the last dimension, each value on 1 to 32 neighbouring positions
- w_query: bfloat16 [4, 4096, 4096], P('section', None, 'tensor'), may hold values from -0.09375 to 0.09375
- w_keyval: bfloat16 [4, 4096, 1024], P('section', None, 'tensor'), may hold values from -0.09375 to 0.09375
- norm_gain: bfloat16 [4, 4096], P('section', 'tensor'), may hold values from 0.5 to 1.5
Outputs:
- grad_query: float32 [4, 4096, 4096], P('section', 'dp', 'tensor')
- grad_keyval: float32 [4, 4096, 1024], P('section', 'dp', 'tensor')
- grad_gains: float32 [4, 4096], P('section', ('tensor', 'dp'))
- layer_input_grads: bfloat16 [4, 16, 2, 64, 4096], P('section', 'dp', None, None, 'tensor')
The draws below stay inside these ranges and needn't reach their ends.
Inputs may be any that keep to these rules, and one draw needn't show every extreme that they name: `segment_ids`: along each sequence the ids never fall.
All inputs are finite; a program needn't handle non-finite values.
Results may differ from the reference program's by a relative error of at most 0.03.
Values may be sent and summed in bfloat16 or wider, within the bound.
A program may use at most 128 MiB of HBM per device.

```python
import math
import jax
import jax.numpy as jnp
import numpy as np
from jax import lax

D = 4096
HD = 128
QH = 32
KVH = 4
L = 64
MB = 2
LAYERS = 4
N_DP = 16


def block_levels(key, shape, pieces, smallest, top_value):
    level = 1.0
    for dim, parts in pieces:
        heights = jax.random.uniform(jax.random.fold_in(jax.random.fold_in(key, 6), dim), (parts,), jnp.float32, smallest / len(pieces), top_value / len(pieces))
        level = level * jnp.repeat(jnp.exp(heights), shape[dim] // parts).reshape((-1,) + (1,) * (len(shape) - 1 - dim))
    return level


def split_up(count, total, most, skew):
    portions = [(1 << 20) // math.isqrt(grade ** skew) + 1 for grade in range(2, count + 1)]
    rest, counts = total - most - (count - 1), [1] * (count - 1)
    while rest > 0:
        candidates = [i for i in range(count - 1) if counts[i] < most]
        mass, left = sum([portions[i] for i in candidates]), rest
        for i in candidates:
            more = min(most - counts[i], max(1, left * portions[i] // mass), rest)
            counts[i] = counts[i] + more
            rest = rest - more
    return np.array([most] + counts)


def uneven_parts(own_key, amount, total, bound, lean):
    if amount == 2:
        one = jax.random.randint(own_key, (), max(1, total - bound), min(bound, total - 1) + 1)
        return jnp.stack([one, total - one])
    sizes = jnp.asarray(split_up(amount, total, bound, lean), jnp.int32)
    couples = (amount - 1) // 2
    donor, taker = sizes[1:1 + 2 * couples:2], sizes[2:2 + 2 * couples:2]
    margin = jnp.minimum(donor - 1, bound - taker)
    shifted = jax.random.randint(jax.random.fold_in(own_key, 1), (couples,), 0, 1 << 20) % (margin + 1)
    sizes = sizes.at[1:1 + 2 * couples:2].set(donor - shifted).at[2:2 + 2 * couples:2].set(taker + shifted)
    return sizes[jax.random.permutation(jax.random.fold_in(own_key, 2), amount)]


def gaussian(rng, extent, spread, bound, cuts=(), kind=jnp.bfloat16):
    drawn = jax.random.normal(rng, extent, jnp.float32) * spread
    if len(cuts) > 0:
        drawn = block_levels(rng, extent, cuts, -0.22, 0.18) * drawn
    return jnp.clip(drawn, min=-bound, max=bound).astype(kind)


def setup_inputs(seed: int = 0) -> dict:
    streams_of = jax.random.split(jax.random.key(seed), 7)
    hidden_in = gaussian(streams_of[0], (N_DP, MB, L, D), 1.0, 6.0, ((0, 16), (3, 4)))
    teacher = gaussian(streams_of[1], (N_DP, MB, L, D), 1.0, 6.0, ((0, 16), (3, 4)))
    segment_ids = jax.vmap(lambda own: jnp.searchsorted(jnp.cumsum(uneven_parts(own, 4, L, L // 2, 1)), jnp.arange(L), side="right"))(jax.random.split(streams_of[2], N_DP * MB)).reshape((N_DP, MB, L)).astype(jnp.int32)
    w_query = gaussian(streams_of[3], (LAYERS, D, QH * HD), D ** -0.5, 0.09375, ((0, 4), (2, 4)))
    w_keyval = gaussian(streams_of[4], (LAYERS, D, KVH * 2 * HD), D ** -0.5, 0.09375, ((0, 4), (2, 4)))
    norm_gain = jnp.clip(1.0 + 0.1 * jax.random.normal(streams_of[5], (LAYERS, D), jnp.float32), 0.5, 1.5).astype(jnp.bfloat16)
    return dict(hidden_in=hidden_in, teacher=teacher, segment_ids=segment_ids, w_query=w_query, w_keyval=w_keyval, norm_gain=norm_gain)


EPSILON = 1e-05

def attend_forward(queries, keyvals, segments, head_size):
    length = queries.shape[0]
    shared_heads = keyvals.shape[1] // (2 * head_size)
    group_size = queries.shape[1] // head_size // shared_heads
    query_heads = queries.astype(jnp.float32).reshape(length, shared_heads, group_size, head_size)
    key_value = keyvals.astype(jnp.float32).reshape(length, shared_heads, 2, head_size)
    score_scale = 1.0 / math.sqrt(head_size)
    scores = jnp.einsum('qhgd,khd->hgqk', query_heads, key_value[:, :, 0]) * score_scale
    query_pos = lax.broadcasted_iota(jnp.int32, (length, length), 0)
    key_pos = lax.broadcasted_iota(jnp.int32, (length, length), 1)
    allowed = (segments[:, None] == segments[None, :]) & (query_pos >= key_pos)
    exponent = jnp.exp(jnp.where(allowed, scores, -jnp.inf))
    probabilities = exponent / lax.optimization_barrier(jnp.sum(exponent, axis=-1, keepdims=True))
    weights = probabilities.astype(jnp.bfloat16)
    heads_out = jnp.einsum('hgqk,khd->qhgd', weights.astype(jnp.float32), key_value[:, :, 1])
    return (heads_out.reshape(length, -1).astype(jnp.bfloat16), probabilities, weights)

def attend_backward(grad_out, queries, keyvals, probabilities, weights, head_size):
    length = queries.shape[0]
    shared_heads = keyvals.shape[1] // (2 * head_size)
    group_size = queries.shape[1] // head_size // shared_heads
    query_heads = queries.astype(jnp.float32).reshape(length, shared_heads, group_size, head_size)
    key_value = keyvals.astype(jnp.float32).reshape(length, shared_heads, 2, head_size)
    grad_heads = grad_out.astype(jnp.float32).reshape(length, shared_heads, group_size, head_size)
    score_scale = 1.0 / math.sqrt(head_size)
    grad_probs = jnp.einsum('qhgd,khd->hgqk', grad_heads, key_value[:, :, 1])
    centered = grad_probs - lax.optimization_barrier(jnp.sum(grad_probs * probabilities, axis=-1, keepdims=True))
    grad_scores = (probabilities * centered).astype(jnp.bfloat16).astype(jnp.float32)
    grad_query = (jnp.einsum('hgqk,khd->qhgd', grad_scores, key_value[:, :, 0]) * score_scale).astype(jnp.bfloat16)
    grad_key = (jnp.einsum('hgqk,qhgd->khd', grad_scores, query_heads) * score_scale).astype(jnp.bfloat16)
    grad_value = jnp.einsum('hgqk,qhgd->khd', weights.astype(jnp.float32), grad_heads).astype(jnp.bfloat16)
    grad_pairs = jnp.stack([grad_key, grad_value], axis=2)
    return (grad_query.reshape(length, -1), grad_pairs.reshape(length, -1))

def rounded(total):
    return lax.optimization_barrier(total.astype(jnp.bfloat16)).astype(jnp.float32)

def reference(hidden_in, teacher, segment_ids, w_query, w_keyval, norm_gain):

    def run_group(running, items):
        inputs, targets, segment_rows = items
        part_query = jnp.zeros(w_query.shape, jnp.float32)
        part_keyval = jnp.zeros(w_keyval.shape, jnp.float32)
        part_gains = jnp.zeros(norm_gain.shape, jnp.float32)
        layer_grads = []
        for micro_index in range(MB):
            hidden = inputs[micro_index]
            segments = segment_rows[micro_index]
            stored = []
            for layer_index in range(LAYERS):
                widened = hidden.astype(jnp.float32)
                inverse = lax.rsqrt(lax.optimization_barrier(jnp.mean(widened * widened, axis=1)) + EPSILON)
                gains = norm_gain[layer_index].astype(jnp.float32)
                normed = (widened * inverse[:, None] * gains).astype(jnp.bfloat16)
                queries = jnp.dot(normed, w_query[layer_index], preferred_element_type=jnp.float32).astype(jnp.bfloat16)
                keyvals = jnp.dot(normed, w_keyval[layer_index], preferred_element_type=jnp.float32).astype(jnp.bfloat16)
                heads_out, probabilities, weights = attend_forward(queries, keyvals, segments, HD)
                stored.append((widened, inverse, normed, queries, keyvals, probabilities, weights))
                hidden = (widened + heads_out.astype(jnp.float32)).astype(jnp.bfloat16)
            grad_hidden = (hidden.astype(jnp.float32) - targets[micro_index].astype(jnp.float32)).astype(jnp.bfloat16)
            per_layer = [None] * LAYERS
            for layer_index in reversed(range(LAYERS)):
                widened, inverse, normed, queries, keyvals, probabilities, weights = stored[layer_index]
                grad_query, grad_keyval = attend_backward(grad_hidden, queries, keyvals, probabilities, weights, HD)
                grad_normed = jnp.dot(grad_query, w_query[layer_index].T, preferred_element_type=jnp.float32)
                grad_normed = grad_normed + jnp.dot(grad_keyval, w_keyval[layer_index].T, preferred_element_type=jnp.float32)
                gains = norm_gain[layer_index].astype(jnp.float32)
                scaled = grad_normed * gains
                row_dots = lax.optimization_barrier(jnp.sum(scaled * widened, axis=1))
                grad_rows = grad_hidden.astype(jnp.float32) + inverse[:, None] * scaled - widened * (inverse ** 3 * row_dots / D)[:, None]
                part_query = part_query.at[layer_index].add(jnp.dot(normed.T, grad_query, preferred_element_type=jnp.float32))
                part_keyval = part_keyval.at[layer_index].add(jnp.dot(normed.T, grad_keyval, preferred_element_type=jnp.float32))
                part_gains = part_gains.at[layer_index].add(lax.optimization_barrier(jnp.sum(grad_normed * widened * inverse[:, None], axis=0)))
                grad_hidden = grad_rows.astype(jnp.bfloat16)
                per_layer[layer_index] = grad_hidden
            layer_grads.append(jnp.stack(per_layer))
        updated = (running[0] + rounded(part_query), running[1] + rounded(part_keyval), running[2] + rounded(part_gains))
        return (updated, jnp.stack(layer_grads, axis=1))
    initial = (jnp.zeros(w_query.shape, jnp.float32), jnp.zeros(w_keyval.shape, jnp.float32), jnp.zeros(norm_gain.shape, jnp.float32))
    totals, stacked = lax.scan(run_group, initial, (hidden_in, teacher, segment_ids))
    return (totals[0], totals[1], totals[2], jnp.transpose(stacked, (1, 0, 2, 3, 4)))
```

```python
import math

import jax
import jax.numpy as jnp
from jax import lax
from jax.experimental import pallas as pl
from jax.experimental.pallas import tpu as pltpu
from jax.sharding import PartitionSpec as P

EPSILON = 1e-05
D = 4096
HD = 128
L = 64
MB = 2
DP = 16
SECTIONS = 4
TENSOR = 4
ROWS = D // DP
QC = 1024
KC = 256
C = QC + KC
BLK = 1024
HB = BLK // 2
BF = jnp.bfloat16
F32 = jnp.float32
MESH = pl.DeviceIdType.MESH
SCALE = 1.0 / math.sqrt(HD)
NT = (((1,), (1,)), ((), ()))
TN = (((0,), (0,)), ((), ()))
NN = (((1,), (0,)), ((), ()))


def dot(a, b, dims=NN):
    return lax.dot_general(a, b, dims, preferred_element_type=F32)


def stack_heads(x):
    return jnp.concatenate([x[:, i * HD : (i + 1) * HD] for i in range(x.shape[1] // HD)], axis=0)


def unstack_heads(x):
    return jnp.concatenate([x[i * L : (i + 1) * L] for i in range(x.shape[0] // L)], axis=1)


def kernel(
    hid, tea, seg, wq, wkv, gain,
    o_gq, o_gkv, o_gg, o_lig,
    w, hbuf, g16, acc, qkv, probs, mask, invb, outb, dyb,
    usend, uall, dqall, msend, mrecv, bsend, asend, abuf, bbuf, bfin, lig, gtot, ggsend, ggrecv,
    w_sem, g_ssem, g_rsem, h_ssem, h_rsem, u_ssem, u_rsem, q_ssem, q_rsem,
    m_ssem, m_rsem, ab_ssem, a_rsem, b_rsem, f_rsem, l_ssem, l_rsem, gg_ssem, gg_rsem,
):
    s = lax.axis_index("section")
    d = lax.axis_index("dp")
    t = lax.axis_index("tensor")
    t1 = t + 1 - 2 * lax.rem(t, 2)
    t2 = lax.rem(t + 2, 4)
    t3 = 3 - t
    z = d // 2
    xl = lax.rem(d, 2)
    sn = lax.rem(s + 1, SECTIONS)
    sp = lax.rem(s + SECTIONS - 1, SECTIONS)

    def rcopy(src, dst, ssem, rsem, dev):
        return pltpu.make_async_remote_copy(
            src_ref=src, dst_ref=dst, send_sem=ssem, recv_sem=rsem, device_id=dev, device_id_type=MESH
        )

    bar = pltpu.get_barrier_semaphore()
    for dev in ((s, d, t1), (s, d, t2), (s, d, t3), (sn, d, t), (sn, d, t2), (sp, d, t), (sp, d, t2)):
        pl.semaphore_signal(bar, inc=1, device_id=dev, device_id_type=MESH)

    def greet(i, _):
        pl.semaphore_signal(bar, inc=1, device_id=(s, lax.rem(d + i, DP), t), device_id_type=MESH)
        return 0

    lax.fori_loop(1, DP, greet, 0)
    gt = d // 4
    src_d = 4 * t + d // 4
    quarter = lax.rem(d, 4)
    loop = (gt == t) & (quarter == gt)
    for tt in range(TENSOR):
        @pl.when(jnp.logical_not(loop & (tt == t)))
        def _():
            pl.semaphore_signal(bar, inc=1, device_id=(s, src_d, tt), device_id_type=MESH)

    def w_copies(j):
        rows = pl.ds(pl.multiple_of(j * BLK, BLK), BLK)
        return (
            pltpu.make_async_copy(wq.at[0, rows, :], w.at[rows, pl.ds(0, QC)], w_sem.at[0, j]),
            pltpu.make_async_copy(wkv.at[0, rows, :], w.at[rows, pl.ds(QC, KC)], w_sem.at[1, j]),
        )

    for j in (t, t1, t2, t3):
        for c in w_copies(j):
            c.start()

    ri = lax.broadcasted_iota(jnp.int32, (L, L), 0)
    ci = lax.broadcasted_iota(jnp.int32, (L, L), 1)
    for m in range(MB):
        srow = jnp.broadcast_to(seg[0, m : m + 1, :], (L, L))
        scol = jnp.sum(jnp.where(ri == ci, srow, 0), axis=1, keepdims=True)
        mask[m] = jnp.where((srow == scol) & (ri >= ci), 1.0, 0.0)
    for i in range(4):
        g16[4 * t + i] = jnp.broadcast_to(gain[:, i * ROWS : (i + 1) * ROWS].astype(F32), (8, ROWS))

    pl.semaphore_wait(bar, 26 - jnp.where(loop, 1, 0))

    def g_copy(i, dev_t):
        sl = g16.at[pl.ds(4 * t, 4)]
        return rcopy(sl, sl, g_ssem.at[i], g_rsem.at[t], (s, d, dev_t))

    def h_copy(m, k, kind, slot, src, dev):
        return rcopy(src, hbuf.at[m, slot, k], h_ssem.at[m, kind, k], h_rsem.at[m, slot, k], dev)

    for i, tt in enumerate((t1, t2, t3)):
        g_copy(i, tt).start()

    @pl.when(s == 0)
    def _():
        for m in range(MB):
            for k in range(2):
                hbuf[m, t, k] = hid[0, m, :, k * HB : (k + 1) * HB]
                h_copy(m, k, 4, t, hbuf.at[m, t, k], (s, d, t2)).start()

    for tt in (t1, t2, t3):
        sl = g16.at[pl.ds(4 * tt, 4)]
        rcopy(sl, sl, g_ssem.at[0], g_rsem.at[tt], (s, d, tt)).wait_recv()

    def gains(j, k):
        p = 4 * j + 2 * k
        return jnp.concatenate([g16[p, 0:1, :], g16[p + 1, 0:1, :]], axis=1)

    def h_wait(m, slot, k):
        h_copy(m, k, 0, slot, hbuf.at[m, slot, k], (s, d, t1)).wait_recv()

    def forward(m):
        ss = jnp.zeros((L, 1), F32)

        def kstep(j, k, first):
            x = hbuf[m, j, k].astype(F32)
            part_ss = jnp.sum(x * x, axis=1, keepdims=True)
            xg = (x * gains(j, k)).astype(BF)
            part = dot(xg, w[pl.ds(pl.multiple_of(j * BLK + k * HB, HB), HB), :])
            if first:
                acc[...] = part
            else:
                acc[...] += part
            return part_ss

        def need_w(j):
            if m == 0:
                for c in w_copies(j):
                    c.wait()

        for k in range(2):
            @pl.when(s > 0)
            def _():
                h_wait(m, t, k)
            h_copy(m, k, 2, t, hbuf.at[m, t, k], (s, d, t1)).start()
        need_w(t)
        for k in range(2):
            ss += kstep(t, k, k == 0)
        for k in range(2):
            h_wait(m, t2, k)
            h_copy(m, k, 3, t2, hbuf.at[m, t2, k], (s, d, t1)).start()
        need_w(t1)
        for k in range(2):
            h_wait(m, t1, k)
            ss += kstep(t1, k, False)
        need_w(t2)
        for k in range(2):
            ss += kstep(t2, k, False)
        need_w(t3)
        for k in range(2):
            h_wait(m, t3, k)
            ss += kstep(t3, k, False)
        inv = lax.rsqrt(ss / D + EPSILON)
        invb[m] = jnp.broadcast_to(inv, (L, 128))
        qkv[m] = (acc[...] * inv).astype(BF)
        key = qkv[m, :, QC : QC + HD]
        val = qkv[m, :, QC + HD :]
        allowed = jnp.concatenate([mask[m]] * 4, axis=0) > 0.0
        for k in range(2):
            q = stack_heads(qkv[m, :, k * HB : (k + 1) * HB])
            sc = dot(q, key, NT) * SCALE
            e = jnp.exp(jnp.where(allowed, sc, -1e30))
            pr = e / jnp.sum(e, axis=1, keepdims=True)
            probs[m, k] = pr
            o = dot(pr.astype(BF), val).astype(BF)
            hn = (hbuf[m, t, k].astype(F32) + unstack_heads(o).astype(F32)).astype(BF)
            outb[m, k] = hn

            @pl.when(s < SECTIONS - 1)
            def _():
                h_copy(m, k, 0, t, outb.at[m, k], (sn, d, t)).start()
                h_copy(m, k, 1, t, outb.at[m, k], (sn, d, t2)).start()

            @pl.when(s == SECTIONS - 1)
            def _():
                dyb[m, k] = (
                    hn.astype(F32) - tea[0, m, :, k * HB : (k + 1) * HB].astype(F32)
                ).astype(BF)

    def u_copy(m, i):
        p = lax.rem(d + i, DP)
        return rcopy(usend.at[m, p], uall.at[m, d], u_ssem.at[m, i], u_rsem.at[m, d], (s, p, t))

    def send_rows(m):
        inv = invb[m, :, 0:1]
        for j in range(TENSOR):
            for k in range(2):
                u = (hbuf[m, j, k].astype(F32) * inv).astype(BF)
                usend[m, 4 * j + 2 * k] = u[:, :ROWS]
                usend[m, 4 * j + 2 * k + 1] = u[:, ROWS:]
        uall[m, d] = usend[m, d]

        def one(i, _):
            u_copy(m, i).start()
            return 0

        lax.fori_loop(1, DP, one, 0)

    def q_copy(m, src_d, sem, dev_d):
        blk = dqall.at[m, src_d]
        return rcopy(blk, blk, q_ssem.at[m, sem], q_rsem.at[m, src_d], (s, dev_d, t))

    dx = d + 1 - 2 * xl
    zr = lax.rem(z + 1, 8)
    zl = lax.rem(z + 7, 8)

    def q_start(m):
        q_copy(m, d, 0, dx).start()
        q_copy(m, d, 1, 2 * zr + xl).start()
        q_copy(m, d, 2, 2 * zl + xl).start()

    def q_wait(m, src_d):
        q_copy(m, src_d, 0, dx).wait_recv()

    def q_hop(m, r, col):
        cx = xl if col == 0 else 1 - xl
        right = 2 * lax.rem(z + 8 - r, 8) + cx
        left = 2 * lax.rem(z + r, 8) + cx
        sem = 1 + 4 * r + 2 * col
        if r > 0 or col == 1:
            q_wait(m, right)
            if r > 0:
                q_wait(m, left)
            if r < 3 or col == 0:
                q_copy(m, right, sem, 2 * zr + xl).start()
            if r < 3 or col == 1:
                q_copy(m, left, sem + 1, 2 * zl + xl).start()

    def q_finish(m):
        for col in range(2):
            q_wait(m, 2 * lax.rem(z + 4, 8) + (xl if col == 0 else 1 - xl))

    def q_drain(m):
        q_copy(m, d, 0, dx).wait_send()
        for r in range(4):
            for col in range(2):
                if r < 3 or col == 0:
                    q_copy(m, d, 1 + 4 * r + 2 * col, dx).wait_send()
                if r < 3 or col == 1:
                    q_copy(m, d, 2 + 4 * r + 2 * col, dx).wait_send()

    def m_copy(m, i, k):
        return rcopy(msend.at[m, i, k], mrecv.at[m, i, k], m_ssem.at[m, i, k], m_rsem.at[m, i, k], (s, d, t1))

    def a_copy(m, k):
        return rcopy(asend.at[m, k], abuf.at[m, k], ab_ssem.at[0, m, k], a_rsem.at[m, k], (sp, d, t))

    def b_copy(m, k):
        return rcopy(bsend.at[m, k], bbuf.at[m, k], ab_ssem.at[1, m, k], b_rsem.at[m, k], (sp, d, t2))

    def f_copy(m, k):
        return rcopy(bsend.at[m, k], bfin.at[m, k], ab_ssem.at[1, m, k], f_rsem.at[m, k], (s, d, t2))

    def l_copy(m, k):
        return rcopy(dyb.at[m, k], lig.at[m, k], l_ssem.at[m, k], l_rsem.at[m, k], (sn, d, t))

    def backward(m):
        key = qkv[m, :, QC : QC + HD]
        val = qkv[m, :, QC + HD :]
        inv = invb[m, :, 0:1]
        dk = jnp.zeros((L, HD), F32)
        dv = jnp.zeros((L, HD), F32)
        rd = jnp.zeros((L, 1), F32)
        for k in range(2):
            @pl.when(s < SECTIONS - 1)
            def _():
                a_copy(m, k).wait_recv()
                b_copy(m, k).wait_recv()
                dyb[m, k] = (abuf[m, k].astype(F32) + bbuf[m, k].astype(F32)).astype(BF)
                l_copy(m, k).start()

            do = stack_heads(dyb[m, k])
            q = stack_heads(qkv[m, :, k * HB : (k + 1) * HB])
            pr = probs[m, k]
            dp = dot(do, val, NT)
            ds = (pr * (dp - jnp.sum(dp * pr, axis=1, keepdims=True))).astype(BF)
            dq = (dot(ds, key) * SCALE).astype(BF)
            dqall[m, d, :, k * HB : (k + 1) * HB] = unstack_heads(dq)
            dk += dot(ds, q, TN)
            dv += dot(pr.astype(BF), do, TN)
            qd = jnp.sum(q.astype(F32) * dq.astype(F32), axis=1, keepdims=True)
            for i in range(4):
                rd += qd[i * L : (i + 1) * L]
        dkb = (dk * SCALE).astype(BF)
        dvb = dv.astype(BF)
        dqall[m, d, :, QC : QC + HD] = dkb
        dqall[m, d, :, QC + HD :] = dvb
        rd += jnp.sum(
            key.astype(F32) * dkb.astype(F32) + val.astype(F32) * dvb.astype(F32), axis=1, keepdims=True
        )
        q_start(m)
        coef = inv * inv * rd / D
        grads = dqall[m, d]

        def term(j, k):
            part = dot(grads, w[pl.ds(pl.multiple_of(j * BLK + k * HB, HB), HB), :], NT)
            return inv * gains(j, k) * part - hbuf[m, j, k].astype(F32) * coef

        for i, j in enumerate((t3, t1)):
            for k in range(2):
                msend[m, i, k] = term(j, k).astype(BF)
                m_copy(m, i, k).start()
        for k in range(2):
            own = term(t2, k)
            m_copy(m, 0, k).wait_recv()
            bsend[m, k] = (own + mrecv[m, 0, k].astype(F32)).astype(BF)

            @pl.when(s > 0)
            def _():
                b_copy(m, k).start()

            @pl.when(s == 0)
            def _():
                f_copy(m, k).start()

        for k in range(2):
            own = term(t, k) + dyb[m, k].astype(F32)
            m_copy(m, 1, k).wait_recv()
            asend[m, k] = (own + mrecv[m, 1, k].astype(F32)).astype(BF)

            @pl.when(s > 0)
            def _():
                a_copy(m, k).start()

    for m in range(MB):
        forward(m)
    for m in range(MB):
        send_rows(m)
    for m in range(MB):
        backward(m)

    for r in range(4):
        for m in range(MB):
            for col in range(2):
                q_hop(m, r, col)

    @pl.when(s == 0)
    def _():
        for m in range(MB):
            for k in range(2):
                f_copy(m, k).wait_recv()
                lig[m, k] = (asend[m, k].astype(F32) + bfin[m, k].astype(F32)).astype(BF)

    @pl.when(s > 0)
    def _():
        for m in range(MB):
            for k in range(2):
                l_copy(m, k).wait_recv()

    for m in range(MB):
        for k in range(2):
            o_lig[0, 0, m, :, k * HB : (k + 1) * HB] = lig[m, k]

    for m in range(MB):
        def u_wait(i, _):
            p = lax.rem(d + i, DP)
            rcopy(usend.at[m, p], uall.at[m, p], u_ssem.at[m, i], u_rsem.at[m, p], (s, p, t)).wait_recv()
            return 0

        lax.fori_loop(1, DP, u_wait, 0)
        q_finish(m)
        u = uall[m].reshape(DP * L, ROWS)
        g = dqall[m].reshape(DP * L, C)
        if m == 0:
            gtot[...] = dot(u, g, TN)
        else:
            gtot[...] += dot(u, g, TN)

    eye = lax.broadcasted_iota(jnp.int32, (ROWS, ROWS), 0) == lax.broadcasted_iota(jnp.int32, (ROWS, ROWS), 1)
    total = gtot[...]
    rows = pl.ds(pl.multiple_of(d * ROWS, ROWS), ROWS)
    col = jnp.sum(total * w[rows, :].astype(F32), axis=1, keepdims=True)
    row = jnp.sum(jnp.where(eye, jnp.broadcast_to(col, (ROWS, ROWS)), 0.0), axis=0, keepdims=True)
    ggsend[...] = jnp.broadcast_to(row, (8, ROWS))

    def gg_copy(j):
        return rcopy(ggsend, ggrecv.at[t], gg_ssem.at[j], gg_rsem.at[t], (s, 4 * quarter + j, gt))

    for j in range(4):
        mine = loop & (quarter == j)

        @pl.when(jnp.logical_not(mine))
        def _():
            gg_copy(j).start()

        @pl.when(mine)
        def _():
            ggrecv[t] = ggsend[...]

    gcol = jnp.sum(
        jnp.where(eye, jnp.broadcast_to(g16[d, 0:1, :], (ROWS, ROWS)), 0.0), axis=1, keepdims=True
    )
    o_gq[0] = total[:, :QC] * gcol
    o_gkv[0] = total[:, QC:] * gcol

    for tt in range(TENSOR):
        @pl.when(jnp.logical_not(loop & (tt == t)))
        def _():
            rcopy(ggsend, ggrecv.at[tt], gg_ssem.at[0], gg_rsem.at[tt], (s, src_d, tt)).wait_recv()
    gsum = ggrecv[0] + ggrecv[1] + ggrecv[2] + ggrecv[3]
    picked = jnp.zeros((1, L), F32)
    for j in range(4):
        picked += jnp.where(quarter == j, 1.0, 0.0) * gsum[0:1, j * L : (j + 1) * L]
    o_gg[...] = picked

    for i, tt in enumerate((t1, t2, t3)):
        g_copy(i, tt).wait_send()
    for m in range(MB):
        for k in range(2):
            h_copy(m, k, 2, t, hbuf.at[m, t, k], (s, d, t1)).wait_send()
            h_copy(m, k, 3, t2, hbuf.at[m, t2, k], (s, d, t1)).wait_send()

            @pl.when(s == 0)
            def _():
                h_copy(m, k, 4, t, hbuf.at[m, t, k], (s, d, t2)).wait_send()

            @pl.when(s < SECTIONS - 1)
            def _():
                h_copy(m, k, 0, t, outb.at[m, k], (sn, d, t)).wait_send()
                h_copy(m, k, 1, t, outb.at[m, k], (sn, d, t2)).wait_send()
                l_copy(m, k).wait_send()

            for i in range(2):
                m_copy(m, i, k).wait_send()
            b_copy(m, k).wait_send()

            @pl.when(s > 0)
            def _():
                a_copy(m, k).wait_send()

        def u_drain(i, _):
            u_copy(m, i).wait_send()
            return 0

        lax.fori_loop(1, DP, u_drain, 0)
        q_drain(m)
    for j in range(4):
        mine = loop & (quarter == j)

        @pl.when(jnp.logical_not(mine))
        def _():
            gg_copy(j).wait_send()


def body(hidden_in, teacher, segment_ids, w_query, w_keyval, norm_gain):
    vmem = pl.BlockSpec(memory_space=pltpu.VMEM)
    hbm = pl.BlockSpec(memory_space=pl.ANY)
    dma = pltpu.SemaphoreType.DMA
    V = pltpu.VMEM
    out = pl.pallas_call(
        kernel,
        out_shape=(
            jax.ShapeDtypeStruct((1, ROWS, QC), F32),
            jax.ShapeDtypeStruct((1, ROWS, KC), F32),
            jax.ShapeDtypeStruct((1, L), F32),
            jax.ShapeDtypeStruct((1, 1, MB, L, BLK), BF),
        ),
        in_specs=[vmem, vmem, vmem, hbm, hbm, vmem],
        out_specs=(vmem, vmem, vmem, vmem),
        scratch_shapes=[
            V((D, C), BF),
            V((MB, TENSOR, 2, L, HB), BF),
            V((DP, 8, ROWS), F32),
            V((L, C), F32),
            V((MB, L, C), BF),
            V((MB, 2, 4 * L, L), F32),
            V((MB, L, L), F32),
            V((MB, L, 128), F32),
            V((MB, 2, L, HB), BF),
            V((MB, 2, L, HB), BF),
            V((MB, DP, L, ROWS), BF),
            V((MB, DP, L, ROWS), BF),
            V((MB, DP, L, C), BF),
            V((MB, 2, 2, L, HB), BF),
            V((MB, 2, 2, L, HB), BF),
            V((MB, 2, L, HB), BF),
            V((MB, 2, L, HB), BF),
            V((MB, 2, L, HB), BF),
            V((MB, 2, L, HB), BF),
            V((MB, 2, L, HB), BF),
            V((MB, 2, L, HB), BF),
            V((ROWS, C), F32),
            V((8, ROWS), F32),
            V((TENSOR, 8, ROWS), F32),
            dma((2, TENSOR)),
            dma((3,)),
            dma((TENSOR,)),
            dma((MB, 5, 2)),
            dma((MB, TENSOR, 2)),
            dma((MB, DP)),
            dma((MB, DP)),
            dma((MB, 17)),
            dma((MB, DP)),
            dma((MB, 2, 2)),
            dma((MB, 2, 2)),
            dma((2, MB, 2)),
            dma((MB, 2)),
            dma((MB, 2)),
            dma((MB, 2)),
            dma((MB, 2)),
            dma((MB, 2)),
            dma((4,)),
            dma((TENSOR,)),
        ],
        compiler_params=pltpu.CompilerParams(
            collective_id=1, has_side_effects=True, vmem_limit_bytes=58 * 1024 * 1024
        ),
        name="train_step",
    )(hidden_in, teacher, segment_ids, w_query, w_keyval, norm_gain)
    return out


def solution(mesh):
    in_specs = (
        P("dp", None, None, "tensor"),
        P("dp", None, None, "tensor"),
        P("dp", None, None),
        P("section", None, "tensor"),
        P("section", None, "tensor"),
        P("section", "tensor"),
    )
    out_specs = (
        P("section", "dp", "tensor"),
        P("section", "dp", "tensor"),
        P("section", ("tensor", "dp")),
        P("section", "dp", None, None, "tensor"),
    )
    return jax.shard_map(body, mesh=mesh, in_specs=in_specs, out_specs=out_specs, check_vma=False)
```

```python
import math

import jax
import jax.numpy as jnp
from jax import lax
from jax.experimental import pallas as pl
from jax.experimental.pallas import tpu as pltpu
from jax.sharding import PartitionSpec as P

EPSILON = 1e-05
D = 4096
HD = 128
L = 64
MB = 2
DP = 16
SECTIONS = 4
TENSOR = 4
ROWS = D // DP
QC = 1024
KC = 256
C = QC + KC
BLK = 1024
HB = BLK // 2
BF = jnp.bfloat16
F32 = jnp.float32
MESH = pl.DeviceIdType.MESH
SCALE = 1.0 / math.sqrt(HD)
NT = (((1,), (1,)), ((), ()))
TN = (((0,), (0,)), ((), ()))
NN = (((1,), (0,)), ((), ()))


def dot(a, b, dims=NN):
    return lax.dot_general(a, b, dims, preferred_element_type=F32)


def place(rz, c):
    rz = rz % 8
    near = 0 if rz == 0 else 2 * rz - 1 if rz <= 4 else 2 * (8 - rz)
    return 2 * near + c


def stack_heads(x):
    return jnp.concatenate([x[:, i * HD : (i + 1) * HD] for i in range(x.shape[1] // HD)], axis=0)


def unstack_heads(x):
    return jnp.concatenate([x[i * L : (i + 1) * L] for i in range(x.shape[0] // L)], axis=1)


def kernel(
    hid, tea, seg, wq, wkv, gain,
    o_gq, o_gkv, o_gg, o_lig,
    w, hbuf, g16, acc, qkv, probs, mask, invb, outb, dyb,
    usend, uall, qown, qs, dqkv, dqall, msend, mrecv, bsend, asend, abuf, bbuf, bfin, lig, gtot, xsend, xrecv, ggsend, ggrecv,
    w_sem, g_ssem, g_rsem, h_ssem, h_rsem, u_ssem, u_rsem, q_ssem, q_rsem,
    m_ssem, m_rsem, ab_ssem, a_rsem, b_rsem, f_rsem, l_ssem, l_rsem, gg_ssem, gg_rsem, x_ssem, x_rsem,
):
    s = lax.axis_index("section")
    d = lax.axis_index("dp")
    t = lax.axis_index("tensor")
    t1 = t + 1 - 2 * lax.rem(t, 2)
    t2 = lax.rem(t + 2, 4)
    t3 = 3 - t
    z = d // 2
    xl = lax.rem(d, 2)
    sn = lax.rem(s + 1, SECTIONS)
    sp = lax.rem(s + SECTIONS - 1, SECTIONS)

    def rcopy(src, dst, ssem, rsem, dev):
        return pltpu.make_async_remote_copy(
            src_ref=src, dst_ref=dst, send_sem=ssem, recv_sem=rsem, device_id=dev, device_id_type=MESH
        )

    bar = pltpu.get_barrier_semaphore()
    for dev in ((s, d, t1), (s, d, t2), (s, d, t3), (sn, d, t), (sn, d, t2), (sp, d, t), (sp, d, t2)):
        pl.semaphore_signal(bar, inc=1, device_id=dev, device_id_type=MESH)

    def greet(i, _):
        pl.semaphore_signal(bar, inc=1, device_id=(s, lax.rem(d + i, DP), t), device_id_type=MESH)
        return 0

    lax.fori_loop(1, DP, greet, 0)
    loop = (t == z // 2) & (z // 4 == lax.rem(z, 2))
    zs = 2 * t + d // 8
    for i in range(8):
        @pl.when(jnp.logical_not(loop & (t == i // 2) & (xl == i % 2)))
        def _():
            pl.semaphore_signal(bar, inc=1, device_id=(s, 2 * zs + i % 2, i // 2), device_id_type=MESH)

    def w_copies(j):
        rows = pl.ds(pl.multiple_of(j * BLK, BLK), BLK)
        return (
            pltpu.make_async_copy(wq.at[0, rows, :], w.at[rows, pl.ds(0, QC)], w_sem.at[0, j]),
            pltpu.make_async_copy(wkv.at[0, rows, :], w.at[rows, pl.ds(QC, KC)], w_sem.at[1, j]),
        )

    for j in (t, t1, t2, t3):
        for c in w_copies(j):
            c.start()

    ri = lax.broadcasted_iota(jnp.int32, (L, L), 0)
    ci = lax.broadcasted_iota(jnp.int32, (L, L), 1)
    for m in range(MB):
        srow = jnp.broadcast_to(seg[0, m : m + 1, :], (L, L))
        scol = jnp.sum(jnp.where(ri == ci, srow, 0), axis=1, keepdims=True)
        mask[m] = jnp.where((srow == scol) & (ri >= ci), 1.0, 0.0)
    for i in range(4):
        g16[4 * t + i] = jnp.broadcast_to(gain[:, i * ROWS : (i + 1) * ROWS].astype(F32), (8, ROWS))

    pl.semaphore_wait(bar, 30 - jnp.where(loop, 1, 0))

    def g_copy(i, dev_t):
        sl = g16.at[pl.ds(4 * t, 4)]
        return rcopy(sl, sl, g_ssem.at[i], g_rsem.at[t], (s, d, dev_t))

    def h_copy(m, k, kind, slot, src, dev):
        return rcopy(src, hbuf.at[m, slot, k], h_ssem.at[m, kind, k], h_rsem.at[m, slot, k], dev)

    for i, tt in enumerate((t1, t2, t3)):
        g_copy(i, tt).start()

    @pl.when(s == 0)
    def _():
        for m in range(MB):
            for k in range(2):
                hbuf[m, t, k] = hid[0, m, :, k * HB : (k + 1) * HB]
                h_copy(m, k, 4, t, hbuf.at[m, t, k], (s, d, t2)).start()

    for tt in (t1, t2, t3):
        sl = g16.at[pl.ds(4 * tt, 4)]
        rcopy(sl, sl, g_ssem.at[0], g_rsem.at[tt], (s, d, tt)).wait_recv()

    def gains(j, k):
        p = 4 * j + 2 * k
        return jnp.concatenate([g16[p, 0:1, :], g16[p + 1, 0:1, :]], axis=1)

    def h_wait(m, slot, k):
        h_copy(m, k, 0, slot, hbuf.at[m, slot, k], (s, d, t1)).wait_recv()

    def forward(m):
        ss = jnp.zeros((L, 1), F32)

        def kstep(j, k, first):
            x = hbuf[m, j, k].astype(F32)
            part_ss = jnp.sum(x * x, axis=1, keepdims=True)
            xg = (x * gains(j, k)).astype(BF)
            part = dot(xg, w[pl.ds(pl.multiple_of(j * BLK + k * HB, HB), HB), :])
            if first:
                acc[...] = part
            else:
                acc[...] += part
            return part_ss

        def need_w(j):
            if m == 0:
                for c in w_copies(j):
                    c.wait()

        for k in range(2):
            @pl.when(s > 0)
            def _():
                h_wait(m, t, k)
            h_copy(m, k, 2, t, hbuf.at[m, t, k], (s, d, t1)).start()
        need_w(t)
        for k in range(2):
            ss += kstep(t, k, k == 0)
        for k in range(2):
            h_wait(m, t2, k)
            h_copy(m, k, 3, t2, hbuf.at[m, t2, k], (s, d, t1)).start()
        need_w(t1)
        for k in range(2):
            h_wait(m, t1, k)
            ss += kstep(t1, k, False)
        need_w(t2)
        for k in range(2):
            ss += kstep(t2, k, False)
        need_w(t3)
        for k in range(2):
            h_wait(m, t3, k)
            ss += kstep(t3, k, False)
        inv = lax.rsqrt(ss / D + EPSILON)
        invb[m] = jnp.broadcast_to(inv, (L, 128))
        qkv[m] = (acc[...] * inv).astype(BF)
        key = qkv[m, :, QC : QC + HD]
        val = qkv[m, :, QC + HD :]
        allowed = jnp.concatenate([mask[m]] * 4, axis=0) > 0.0
        for k in range(2):
            q = stack_heads(qkv[m, :, k * HB : (k + 1) * HB])
            sc = dot(q, key, NT) * SCALE
            e = jnp.exp(jnp.where(allowed, sc, -1e30))
            pr = e / jnp.sum(e, axis=1, keepdims=True)
            probs[m, k] = pr
            o = dot(pr.astype(BF), val).astype(BF)
            hn = (hbuf[m, t, k].astype(F32) + unstack_heads(o).astype(F32)).astype(BF)
            outb[m, k] = hn

            @pl.when(s < SECTIONS - 1)
            def _():
                h_copy(m, k, 0, t, outb.at[m, k], (sn, d, t)).start()
                h_copy(m, k, 1, t, outb.at[m, k], (sn, d, t2)).start()

            @pl.when(s == SECTIONS - 1)
            def _():
                dyb[m, k] = (
                    hn.astype(F32) - tea[0, m, :, k * HB : (k + 1) * HB].astype(F32)
                ).astype(BF)

    def peer(rz, c):
        return (s, 2 * lax.rem(z + rz % 8, 8) + (1 - xl if c else xl), t)

    def u_copy(m, rz):
        slot = place(-rz, 0) if rz else place(0, 1)
        src = usend.at[m, lax.rem(z + rz, 8) if rz else z]
        return rcopy(src, uall.at[m, slot], u_ssem.at[m, slot], u_rsem.at[m, slot], peer(rz, 0 if rz else 1))

    def u_pass_copy(m, rz):
        slot = place(rz, 1)
        return rcopy(
            uall.at[m, place(rz, 0)], uall.at[m, slot], u_ssem.at[m, slot], u_rsem.at[m, slot], peer(0, 1)
        )

    def u_pass(m):
        for rz in (1, 7, 2, 6, 3, 5, 4):
            u_wait_one(m, place(rz, 0))
            u_pass_copy(m, rz).start()

    def u_wait_one(m, i):
        blk = uall.at[m, i]
        rcopy(blk, blk, u_ssem.at[m, i], u_rsem.at[m, i], peer(1, 0)).wait_recv()

    def send_rows(m):
        inv = invb[m, :, 0:1]
        for j in range(TENSOR):
            for k in range(2):
                u = (hbuf[m, j, k].astype(F32) * inv).astype(BF)
                for i in range(4):
                    usend[m, 2 * j + k, i] = u[:, i * HD : (i + 1) * HD]
        for p in range(8):
            usend[m, p, 4] = qkv[m, :, QC : QC + HD]
        uall[m, 0] = usend[m, z]
        for rz in (0, 1, 7, 2, 6, 3, 5, 4):
            u_copy(m, rz).start()


    def q_copy(m, src, rz, c, step, dc):
        dst = place(rz - step, c ^ dc)
        return rcopy(src, qs.at[m, dst], q_ssem.at[m, dst], q_rsem.at[m, dst], peer(step, dc))

    def q_wait(m, rz, c):
        blk = qs.at[m, place(rz, c)]
        rcopy(blk, blk, q_ssem.at[m, 0], q_rsem.at[m, place(rz, c)], peer(1, 0)).wait_recv()

    def q_start(m):
        qs[m, 0] = qown[m, xl]
        for step in (2, 6, 1, 7, 0):
            for c in range(2):
                if step or c:
                    q_copy(m, qown.at[m, 1 - xl if c else xl], 0, 0, step, c).start()

    def q_hop(m):
        for c in range(2):
            for sg in (1, -1):
                q_wait(m, -2 * sg, c)
                src = qs.at[m, place(-2 * sg, c)]
                q_copy(m, src, -2 * sg, c, sg, 0).start()
                if c == (0 if sg == 1 else 1):
                    q_copy(m, src, -2 * sg, c, 2 * sg, 0).start()

    def q_near(m):
        for rz, c in ((0, 1), (1, 0), (-1, 0), (1, 1), (-1, 1)):
            q_wait(m, rz, c)

    def q_far(m):
        for rz in (3, -3, 4):
            for c in range(2):
                q_wait(m, rz, c)

    def q_make(m, lo, hi):
        for i in range(lo, hi):
            keys = uall[m, i, 4]
            none = jnp.zeros_like(keys)
            pair = jnp.concatenate(
                [jnp.concatenate([keys, none], axis=1), jnp.concatenate([none, keys], axis=1)], axis=0
            )
            dq = (dot(qs[m, i, : 2 * L, :], pair) * SCALE).astype(BF)
            for h in range(4):
                dqall[m, i, :, h * HD : (h + 1) * HD] = dq[
                    (h % 2) * L : (h % 2 + 1) * L, (h // 2) * HD : (h // 2 + 1) * HD
                ]
            dqall[m, i, :, HB:] = qs[m, i, 2 * L :, :]

    def q_drain(m):
        for i in range(1, DP):
            blk = qs.at[m, i]
            rcopy(blk, blk, q_ssem.at[m, i], q_rsem.at[m, i], peer(1, 0)).wait_send()

    def m_copy(m, i, k):
        return rcopy(msend.at[m, i, k], mrecv.at[m, i, k], m_ssem.at[m, i, k], m_rsem.at[m, i, k], (s, d, t1))

    def a_copy(m, k):
        return rcopy(asend.at[m, k], abuf.at[m, k], ab_ssem.at[0, m, k], a_rsem.at[m, k], (sp, d, t))

    def b_copy(m, k):
        return rcopy(bsend.at[m, k], bbuf.at[m, k], ab_ssem.at[1, m, k], b_rsem.at[m, k], (sp, d, t2))

    def f_copy(m, k):
        return rcopy(bsend.at[m, k], bfin.at[m, k], ab_ssem.at[1, m, k], f_rsem.at[m, k], (s, d, t2))

    def l_copy(m, k):
        return rcopy(dyb.at[m, k], lig.at[m, k], l_ssem.at[m, k], l_rsem.at[m, k], (sn, d, t))

    def early_hop():
        @pl.when(s == 0)
        def _():
            q_hop(0)

    def backward(m):
        key = qkv[m, :, QC : QC + HD]
        val = qkv[m, :, QC + HD :]
        inv = invb[m, :, 0:1]
        dk = jnp.zeros((L, HD), F32)
        dv = jnp.zeros((L, HD), F32)
        rd = jnp.zeros((L, 1), F32)
        for k in range(2):
            @pl.when(s < SECTIONS - 1)
            def _():
                a_copy(m, k).wait_recv()
                b_copy(m, k).wait_recv()
                dyb[m, k] = (abuf[m, k].astype(F32) + bbuf[m, k].astype(F32)).astype(BF)
                l_copy(m, k).start()

            do = stack_heads(dyb[m, k])
            q = stack_heads(qkv[m, :, k * HB : (k + 1) * HB])
            pr = probs[m, k]
            dp = dot(do, val, NT)
            ds = (pr * (dp - jnp.sum(dp * pr, axis=1, keepdims=True))).astype(BF)
            dq = (dot(ds, key) * SCALE).astype(BF)
            dqkv[m, :, k * HB : (k + 1) * HB] = unstack_heads(dq)
            qown[m, k, : 2 * L, :L] = ds[: 2 * L]
            qown[m, k, : 2 * L, L:] = ds[2 * L :]
            dk += dot(ds, q, TN)
            dv += dot(pr.astype(BF), do, TN)
            qd = jnp.sum(q.astype(F32) * dq.astype(F32), axis=1, keepdims=True)
            for i in range(4):
                rd += qd[i * L : (i + 1) * L]
        dkb = (dk * SCALE).astype(BF)
        dvb = dv.astype(BF)
        dqkv[m, :, QC : QC + HD] = dkb
        dqkv[m, :, QC + HD :] = dvb
        qown[m, 0, 2 * L :, :] = dkb
        qown[m, 1, 2 * L :, :] = dvb
        rd += jnp.sum(
            key.astype(F32) * dkb.astype(F32) + val.astype(F32) * dvb.astype(F32), axis=1, keepdims=True
        )
        q_start(m)
        if m == 1:
            early_hop()
        coef = inv * inv * rd / D
        grads = dqkv[m]

        def term(j, k):
            part = dot(grads, w[pl.ds(pl.multiple_of(j * BLK + k * HB, HB), HB), :], NT)
            return inv * gains(j, k) * part - hbuf[m, j, k].astype(F32) * coef

        for i, j in enumerate((t3, t1)):
            for k in range(2):
                msend[m, i, k] = term(j, k).astype(BF)
                m_copy(m, i, k).start()
        for k in range(2):
            own = term(t2, k)
            m_copy(m, 0, k).wait_recv()
            bsend[m, k] = (own + mrecv[m, 0, k].astype(F32)).astype(BF)

            @pl.when(s > 0)
            def _():
                b_copy(m, k).start()

            @pl.when(s == 0)
            def _():
                f_copy(m, k).start()

        for k in range(2):
            own = term(t, k) + dyb[m, k].astype(F32)
            m_copy(m, 1, k).wait_recv()
            asend[m, k] = (own + mrecv[m, 1, k].astype(F32)).astype(BF)

            @pl.when(s > 0)
            def _():
                a_copy(m, k).start()

    for m in range(MB):
        forward(m)

    @pl.when(s < SECTIONS - 1)
    def _():
        for m in range(MB):
            send_rows(m)

    @pl.when(s < 2)
    def _():
        for m in range(MB):
            u_pass(m)

    backward(0)
    backward(1)

    @pl.when(s == SECTIONS - 1)
    def _():
        for m in range(MB):
            send_rows(m)

    @pl.when(s > 0)
    def _():
        q_hop(0)

    @pl.when(s >= 2)
    def _():
        for m in range(MB):
            u_pass(m)

    def u_wait(m):
        for rz in range(8):
            u_wait_one(m, place(rz, 1))

    def weight_grads(m, lo, hi, block, i):
        u = uall[m, lo:hi, 2 * block + i].reshape((hi - lo) * L, HD)
        g = dqall[m, lo:hi].reshape((hi - lo) * L, HB + HD)
        part = dot(u, g, TN)
        if m == 0 and lo == 0:
            gtot[block, i] = part
        else:
            gtot[block, i] += part

    u_wait(0)
    q_near(0)
    q_make(0, 0, 10)
    q_hop(1)
    u_wait(1)
    q_far(0)
    q_make(0, 10, DP)
    q_near(1)
    q_make(1, 0, 10)
    for block in range(2):
        for i in range(2):
            weight_grads(0, 0, DP, block, i)
            weight_grads(1, 0, 10, block, i)

    @pl.when(s == 0)
    def _():
        for m in range(MB):
            for k in range(2):
                f_copy(m, k).wait_recv()
                lig[m, k] = (asend[m, k].astype(F32) + bfin[m, k].astype(F32)).astype(BF)

    @pl.when(s > 0)
    def _():
        for m in range(MB):
            for k in range(2):
                l_copy(m, k).wait_recv()

    for m in range(MB):
        for k in range(2):
            o_lig[0, 0, m, :, k * HB : (k + 1) * HB] = lig[m, k]

    q_far(1)
    q_make(1, 10, DP)

    def x_copy(i):
        return rcopy(xsend.at[i], xrecv.at[i], x_ssem.at[i], x_rsem.at[i], peer(0, 1))

    for i in range(2):
        weight_grads(1, 10, DP, 1 - xl, i)
        xsend[i] = gtot[1 - xl, i].astype(BF)
        x_copy(i).start()
    for i in range(2):
        weight_grads(1, 10, DP, xl, i)

    eye = lax.broadcasted_iota(jnp.int32, (HD, HD), 0) == lax.broadcasted_iota(jnp.int32, (HD, HD), 1)
    for block in range(2):
        for i in range(2):
            rows = pl.ds(pl.multiple_of((2 * z + block) * ROWS + i * HD, HD), HD)
            wide = w[rows, pl.ds(pl.multiple_of(xl * HB, HB), HB)].astype(F32)
            narrow = w[rows, pl.ds(pl.multiple_of(QC + xl * HD, HD), HD)].astype(F32)
            total = gtot[block, i]
            col = jnp.sum(total[:, :HB] * wide, axis=1, keepdims=True) + jnp.sum(
                total[:, HB:] * narrow, axis=1, keepdims=True
            )
            row = jnp.sum(jnp.where(eye, jnp.broadcast_to(col, (HD, HD)), 0.0), axis=0, keepdims=True)
            ggsend[block, :, i * HD : (i + 1) * HD] = jnp.broadcast_to(row, (8, HD))

    def gg_copy(block, j):
        n = 4 * block + j
        src = 2 * t + xl
        return rcopy(
            ggsend.at[block], ggrecv.at[src], gg_ssem.at[n], gg_rsem.at[src], (s, 8 * lax.rem(z, 2) + n, z // 2)
        )

    for block in range(2):
        for j in range(4):
            mine = loop & (lax.rem(d, 8) == 4 * block + j)

            @pl.when(jnp.logical_not(mine))
            def _():
                gg_copy(block, j).start()

            @pl.when(mine)
            def _():
                ggrecv[2 * t + xl] = ggsend[block]

    for i in range(2):
        x_copy(i).wait_recv()
        grow = g16[d, 0:1, i * HD : (i + 1) * HD]
        gcol = jnp.sum(jnp.where(eye, jnp.broadcast_to(grow, (HD, HD)), 0.0), axis=1, keepdims=True)
        own = gtot[xl, i]
        other = xrecv[i].astype(F32)
        first = jnp.where(xl == 0, own, other) * gcol
        second = jnp.where(xl == 0, other, own) * gcol
        rs = slice(i * HD, (i + 1) * HD)
        o_gq[0, rs, :HB] = first[:, :HB]
        o_gq[0, rs, HB:] = second[:, :HB]
        o_gkv[0, rs, :HD] = first[:, HB:]
        o_gkv[0, rs, HD:] = second[:, HB:]

    gsum = jnp.zeros((8, ROWS), F32)
    for i in range(8):
        @pl.when(jnp.logical_not(loop & (t == i // 2) & (xl == i % 2)))
        def _():
            rcopy(
                ggsend.at[0], ggrecv.at[i], gg_ssem.at[0], gg_rsem.at[i], (s, 2 * zs + i % 2, i // 2)
            ).wait_recv()
        gsum += ggrecv[i]
    quarter = lax.rem(d, 4)
    picked = jnp.zeros((1, L), F32)
    for j in range(4):
        picked += jnp.where(quarter == j, 1.0, 0.0) * gsum[0:1, j * L : (j + 1) * L]
    o_gg[...] = picked

    for i, tt in enumerate((t1, t2, t3)):
        g_copy(i, tt).wait_send()
    for m in range(MB):
        for k in range(2):
            h_copy(m, k, 2, t, hbuf.at[m, t, k], (s, d, t1)).wait_send()
            h_copy(m, k, 3, t2, hbuf.at[m, t2, k], (s, d, t1)).wait_send()

            @pl.when(s == 0)
            def _():
                h_copy(m, k, 4, t, hbuf.at[m, t, k], (s, d, t2)).wait_send()

            @pl.when(s < SECTIONS - 1)
            def _():
                h_copy(m, k, 0, t, outb.at[m, k], (sn, d, t)).wait_send()
                h_copy(m, k, 1, t, outb.at[m, k], (sn, d, t2)).wait_send()
                l_copy(m, k).wait_send()

            for i in range(2):
                m_copy(m, i, k).wait_send()
            b_copy(m, k).wait_send()

            @pl.when(s > 0)
            def _():
                a_copy(m, k).wait_send()

        for rz in range(8):
            u_copy(m, rz).wait_send()
            if rz:
                u_pass_copy(m, rz).wait_send()
        q_drain(m)
    for i in range(2):
        x_copy(i).wait_send()
    for block in range(2):
        for j in range(4):
            @pl.when(jnp.logical_not(loop & (lax.rem(d, 8) == 4 * block + j)))
            def _():
                gg_copy(block, j).wait_send()


def hand_out(*refs):
    for i in range(4):
        refs[4 + i][...] = refs[i][...]


def body(hidden_in, teacher, segment_ids, w_query, w_keyval, norm_gain):
    vmem = pl.BlockSpec(memory_space=pltpu.VMEM)
    hbm = pl.BlockSpec(memory_space=pl.ANY)
    dma = pltpu.SemaphoreType.DMA
    V = pltpu.VMEM
    out = pl.pallas_call(
        kernel,
        out_shape=(
            jax.ShapeDtypeStruct((1, ROWS, QC), F32),
            jax.ShapeDtypeStruct((1, ROWS, KC), F32),
            jax.ShapeDtypeStruct((1, L), F32),
            jax.ShapeDtypeStruct((1, 1, MB, L, BLK), BF),
        ),
        in_specs=[vmem, vmem, vmem, hbm, hbm, vmem],
        out_specs=(vmem, vmem, vmem, vmem),
        scratch_shapes=[
            V((D, C), BF),
            V((MB, TENSOR, 2, L, HB), BF),
            V((DP, 8, ROWS), F32),
            V((L, C), F32),
            V((MB, L, C), BF),
            V((MB, 2, 4 * L, L), F32),
            V((MB, L, L), F32),
            V((MB, L, 128), F32),
            V((MB, 2, L, HB), BF),
            V((MB, 2, L, HB), BF),
            V((MB, 8, 5, L, HD), BF),
            V((MB, DP, 5, L, HD), BF),
            V((MB, 2, 3 * L, HD), BF),
            V((MB, DP, 3 * L, HD), BF),
            V((MB, L, C), BF),
            V((MB, DP, L, HB + HD), BF),
            V((MB, 2, 2, L, HB), BF),
            V((MB, 2, 2, L, HB), BF),
            V((MB, 2, L, HB), BF),
            V((MB, 2, L, HB), BF),
            V((MB, 2, L, HB), BF),
            V((MB, 2, L, HB), BF),
            V((MB, 2, L, HB), BF),
            V((MB, 2, L, HB), BF),
            V((2, 2, HD, HB + HD), F32),
            V((2, HD, HB + HD), BF),
            V((2, HD, HB + HD), BF),
            V((2, 8, ROWS), F32),
            V((8, 8, ROWS), F32),
            dma((2, TENSOR)),
            dma((3,)),
            dma((TENSOR,)),
            dma((MB, 5, 2)),
            dma((MB, TENSOR, 2)),
            dma((MB, DP)),
            dma((MB, DP)),
            dma((MB, DP)),
            dma((MB, DP)),
            dma((MB, 2, 2)),
            dma((MB, 2, 2)),
            dma((2, MB, 2)),
            dma((MB, 2)),
            dma((MB, 2)),
            dma((MB, 2)),
            dma((MB, 2)),
            dma((MB, 2)),
            dma((8,)),
            dma((8,)),
            dma((2,)),
            dma((2,)),
        ],
        compiler_params=pltpu.CompilerParams(
            collective_id=1, has_side_effects=True, vmem_limit_bytes=58 * 1024 * 1024
        ),
        name="train_step",
    )(hidden_in, teacher, segment_ids, w_query, w_keyval, norm_gain)
    return pl.pallas_call(
        hand_out,
        out_shape=tuple(jax.ShapeDtypeStruct(o.shape, o.dtype) for o in out),
        in_specs=[vmem] * 4,
        out_specs=(vmem,) * 4,
        name="hand_out",
    )(*out)


def solution(mesh):
    in_specs = (
        P("dp", None, None, "tensor"),
        P("dp", None, None, "tensor"),
        P("dp", None, None),
        P("section", None, "tensor"),
        P("section", None, "tensor"),
        P("section", "tensor"),
    )
    out_specs = (
        P("section", "dp", "tensor"),
        P("section", "dp", "tensor"),
        P("section", ("tensor", "dp")),
        P("section", "dp", None, None, "tensor"),
    )
    return jax.shard_map(body, mesh=mesh, in_specs=in_specs, out_specs=out_specs, check_vma=False)
```

```python
import math

import jax
import jax.numpy as jnp
from jax import lax
from jax.experimental import pallas as pl
from jax.experimental.pallas import tpu as pltpu
from jax.sharding import PartitionSpec as P

EPSILON = 1e-05
D = 4096
HD = 128
L = 64
W = 32
MB = 2
DP = 16
SECTIONS = 4
TENSOR = 4
ROWS = D // DP
QC = 1024
KC = 256
C = QC + KC
BLK = 1024
HB = BLK // 2
BF = jnp.bfloat16
F32 = jnp.float32
MESH = pl.DeviceIdType.MESH
SCALE = 1.0 / math.sqrt(HD)
NT = (((1,), (1,)), ((), ()))
TN = (((0,), (0,)), ((), ()))
NN = (((1,), (0,)), ((), ()))


def dot(a, b, dims=NN):
    return lax.dot_general(a, b, dims, preferred_element_type=F32)


def place(rz, c):
    rz = rz % 8
    near = 0 if rz == 0 else 2 * rz - 1 if rz <= 4 else 2 * (8 - rz)
    return 2 * near + c


def stack_heads(x):
    return jnp.concatenate([x[:, i * HD : (i + 1) * HD] for i in range(x.shape[1] // HD)], axis=0)


def unstack_heads(x):
    return jnp.concatenate([x[i * L : (i + 1) * L] for i in range(x.shape[0] // L)], axis=1)


def kernel(
    hid, tea, seg, wq, wkv, gain,
    o_gq, o_gkv, o_gg, o_lig,
    w, hbuf, g16, acc, qkv, probs, mask, invb, outb, dyb,
    usend, uall, qown, qs, low, kdiag, dqkv, dqall, msend, mrecv, bsend, asend, abuf, bbuf, bfin, lig, gtot, xsend, xrecv, ggsend, ggrecv,
    w_sem, g_ssem, g_rsem, h_ssem, h_rsem, u_ssem, u_rsem, q_ssem, q_rsem,
    m_ssem, m_rsem, ab_ssem, a_rsem, b_rsem, f_rsem, l_ssem, l_rsem, gg_ssem, gg_rsem, x_ssem, x_rsem,
):
    s = lax.axis_index("section")
    d = lax.axis_index("dp")
    t = lax.axis_index("tensor")
    t1 = t + 1 - 2 * lax.rem(t, 2)
    t2 = lax.rem(t + 2, 4)
    t3 = 3 - t
    z = d // 2
    xl = lax.rem(d, 2)
    sn = lax.rem(s + 1, SECTIONS)
    sp = lax.rem(s + SECTIONS - 1, SECTIONS)

    def rcopy(src, dst, ssem, rsem, dev):
        return pltpu.make_async_remote_copy(
            src_ref=src, dst_ref=dst, send_sem=ssem, recv_sem=rsem, device_id=dev, device_id_type=MESH
        )

    bar = pltpu.get_barrier_semaphore()
    for dev in ((s, d, t1), (s, d, t2), (s, d, t3), (sn, d, t), (sn, d, t2), (sp, d, t), (sp, d, t2)):
        pl.semaphore_signal(bar, inc=1, device_id=dev, device_id_type=MESH)

    def greet(i, _):
        pl.semaphore_signal(bar, inc=1, device_id=(s, lax.rem(d + i, DP), t), device_id_type=MESH)
        return 0

    lax.fori_loop(1, DP, greet, 0)
    loop = (t == z // 2) & (z // 4 == lax.rem(z, 2))
    zs = 2 * t + d // 8
    for i in range(8):
        @pl.when(jnp.logical_not(loop & (t == i // 2) & (xl == i % 2)))
        def _():
            pl.semaphore_signal(bar, inc=1, device_id=(s, 2 * zs + i % 2, i // 2), device_id_type=MESH)

    def w_copies(j):
        rows = pl.ds(pl.multiple_of(j * BLK, BLK), BLK)
        return (
            pltpu.make_async_copy(wq.at[0, rows, :], w.at[rows, pl.ds(0, QC)], w_sem.at[0, j]),
            pltpu.make_async_copy(wkv.at[0, rows, :], w.at[rows, pl.ds(QC, KC)], w_sem.at[1, j]),
        )

    for j in (t, t2, t1, t3):
        for c in w_copies(j):
            c.start()

    ri = lax.broadcasted_iota(jnp.int32, (L, L), 0)
    ci = lax.broadcasted_iota(jnp.int32, (L, L), 1)
    for m in range(MB):
        srow = jnp.broadcast_to(seg[0, m : m + 1, :], (L, L))
        scol = jnp.sum(jnp.where(ri == ci, srow, 0), axis=1, keepdims=True)
        mask[m] = jnp.where((srow == scol) & (ri >= ci), 1.0, 0.0)
    fi = lax.broadcasted_iota(jnp.int32, (L, HD), 0)
    fj = lax.rem(lax.broadcasted_iota(jnp.int32, (L, HD), 1), W)
    low[0] = jnp.where(fj > fi - W, 1.0, 0.0).astype(BF)
    low[1] = jnp.where(fj > fi - W, 0.0, 1.0).astype(BF)
    kdiag[...] = jnp.zeros_like(kdiag)
    for i in range(4):
        g16[4 * t + i] = jnp.broadcast_to(gain[:, i * ROWS : (i + 1) * ROWS].astype(F32), (8, ROWS))

    pl.semaphore_wait(bar, 30 - jnp.where(loop, 1, 0))

    def g_copy(i, dev_t):
        sl = g16.at[pl.ds(4 * t, 4)]
        return rcopy(sl, sl, g_ssem.at[i], g_rsem.at[t], (s, d, dev_t))

    def h_copy(m, k, kind, slot, src, dev):
        return rcopy(src, hbuf.at[m, slot, k], h_ssem.at[m, kind, k], h_rsem.at[m, slot, k], dev)

    for i, tt in enumerate((t1, t2, t3)):
        g_copy(i, tt).start()

    @pl.when(s == 0)
    def _():
        for m in range(MB):
            for k in range(2):
                hbuf[m, t, k] = hid[0, m, :, k * HB : (k + 1) * HB]
                h_copy(m, k, 4, t, hbuf.at[m, t, k], (s, d, t2)).start()

    for tt in (t1, t2, t3):
        sl = g16.at[pl.ds(4 * tt, 4)]
        rcopy(sl, sl, g_ssem.at[0], g_rsem.at[tt], (s, d, tt)).wait_recv()

    def gains(j, k):
        p = 4 * j + 2 * k
        return jnp.concatenate([g16[p, 0:1, :], g16[p + 1, 0:1, :]], axis=1)

    def h_wait(m, slot, k):
        h_copy(m, k, 0, slot, hbuf.at[m, slot, k], (s, d, t1)).wait_recv()

    def forward(m):
        ss = jnp.zeros((L, 1), F32)

        def kstep(j, k, first):
            x = hbuf[m, j, k].astype(F32)
            part_ss = jnp.sum(x * x, axis=1, keepdims=True)
            xg = (x * gains(j, k)).astype(BF)
            part = dot(xg, w[pl.ds(pl.multiple_of(j * BLK + k * HB, HB), HB), :])
            if first:
                acc[...] = part
            else:
                acc[...] += part
            return part_ss

        def need_w(j):
            if m == 0:
                for c in w_copies(j):
                    c.wait()

        def arrive(k):
            @pl.when(s > 0)
            def _():
                h_wait(m, t, k)
            h_copy(m, k, 2, t, hbuf.at[m, t, k], (s, d, t1)).start()
            h_wait(m, t2, k)
            h_copy(m, k, 3, t2, hbuf.at[m, t2, k], (s, d, t1)).start()

        arrive(0)
        need_w(t)
        ss += kstep(t, 0, True)
        need_w(t2)
        ss += kstep(t2, 0, False)
        arrive(1)
        need_w(t1)
        h_wait(m, t1, 0)
        ss += kstep(t1, 0, False)
        need_w(t3)
        h_wait(m, t3, 0)
        ss += kstep(t3, 0, False)
        ss += kstep(t, 1, False)
        ss += kstep(t2, 1, False)
        h_wait(m, t1, 1)
        ss += kstep(t1, 1, False)
        h_wait(m, t3, 1)
        ss += kstep(t3, 1, False)
        inv = lax.rsqrt(ss / D + EPSILON)
        invb[m] = jnp.broadcast_to(inv, (L, 128))
        qkv[m] = (acc[...] * inv).astype(BF)
        key = qkv[m, :, QC : QC + HD]
        val = qkv[m, :, QC + HD :]
        allowed = jnp.concatenate([mask[m]] * 4, axis=0) > 0.0
        for k in range(2):
            q = stack_heads(qkv[m, :, k * HB : (k + 1) * HB])
            sc = dot(q, key, NT) * SCALE
            e = jnp.exp(jnp.where(allowed, sc, -1e30))
            pr = e / jnp.sum(e, axis=1, keepdims=True)
            probs[m, k] = pr
            o = dot(pr.astype(BF), val).astype(BF)
            hn = (hbuf[m, t, k].astype(F32) + unstack_heads(o).astype(F32)).astype(BF)
            outb[m, k] = hn

            @pl.when(s < SECTIONS - 1)
            def _():
                h_copy(m, k, 0, t, outb.at[m, k], (sn, d, t)).start()
                h_copy(m, k, 1, t, outb.at[m, k], (sn, d, t2)).start()

            @pl.when(s == SECTIONS - 1)
            def _():
                dyb[m, k] = (
                    hn.astype(F32) - tea[0, m, :, k * HB : (k + 1) * HB].astype(F32)
                ).astype(BF)

    def peer(rz, c):
        return (s, 2 * lax.rem(z + rz % 8, 8) + (1 - xl if c else xl), t)

    def u_copy(m, rz):
        slot = place(-rz, 0) if rz else place(0, 1)
        src = usend.at[m, lax.rem(z + rz, 8) if rz else z]
        return rcopy(src, uall.at[m, slot], u_ssem.at[m, slot], u_rsem.at[m, slot], peer(rz, 0 if rz else 1))

    def u_pass_copy(m, rz):
        slot = place(rz, 1)
        return rcopy(
            uall.at[m, place(rz, 0)], uall.at[m, slot], u_ssem.at[m, slot], u_rsem.at[m, slot], peer(0, 1)
        )

    def u_pass(m):
        for rz in (1, 7, 2, 6, 3, 5, 4):
            u_wait_one(m, place(rz, 0))
            u_pass_copy(m, rz).start()

    def u_wait_one(m, i):
        blk = uall.at[m, i]
        rcopy(blk, blk, u_ssem.at[m, i], u_rsem.at[m, i], peer(1, 0)).wait_recv()

    def send_rows(m):
        inv = invb[m, :, 0:1]
        for j in range(TENSOR):
            for k in range(2):
                u = (hbuf[m, j, k].astype(F32) * inv).astype(BF)
                for i in range(4):
                    usend[m, 2 * j + k, i] = u[:, i * HD : (i + 1) * HD]
        for p in range(8):
            usend[m, p, 4] = qkv[m, :, QC : QC + HD]
        uall[m, 0] = usend[m, z]
        for rz in (0, 1, 7, 2, 6, 3, 5, 4):
            u_copy(m, rz).start()


    def q_copy(m, src, rz, c, step, dc):
        dst = place(rz - step, c ^ dc)
        return rcopy(src, qs.at[m, dst], q_ssem.at[m, dst], q_rsem.at[m, dst], peer(step, dc))

    def q_wait(m, rz, c):
        blk = qs.at[m, place(rz, c)]
        rcopy(blk, blk, q_ssem.at[m, 0], q_rsem.at[m, place(rz, c)], peer(1, 0)).wait_recv()

    def q_start(m):
        qs[m, 0] = qown[m, xl]
        for step in (2, 6, 1, 7, 0):
            for c in range(2):
                if step or c:
                    q_copy(m, qown.at[m, 1 - xl if c else xl], 0, 0, step, c).start()

    def q_hop(m):
        for c in range(2):
            for sg in (1, -1):
                q_wait(m, -2 * sg, c)
                src = qs.at[m, place(-2 * sg, c)]
                q_copy(m, src, -2 * sg, c, sg, 0).start()
                if c == (0 if sg == 1 else 1):
                    q_copy(m, src, -2 * sg, c, 2 * sg, 0).start()

    def q_near(m):
        for rz, c in ((0, 1), (1, 0), (-1, 0), (1, 1), (-1, 1)):
            q_wait(m, rz, c)

    def q_far(m):
        for rz in (3, -3, 4):
            for c in range(2):
                q_wait(m, rz, c)

    def q_make(m, lo, hi):
        for i in range(lo, hi):
            pair = kdiag.at[i % 2]
            for h in range(4):
                pair[h * W : (h + 1) * W, h * HD : (h + 1) * HD] = uall[m, i, 4, :W]
                pair[HD + h * W : HD + (h + 1) * W, h * HD : (h + 1) * HD] = uall[m, i, 4, W:]
            fold = qs[m, i, :L, :]
            both = jnp.concatenate([fold * low[0], fold * low[1]], axis=1)
            dqall[m, i, :, :HB] = (dot(both, pair[...]) * SCALE).astype(BF)
            dqall[m, i, :, HB:] = qs[m, i, L:, :]

    def q_drain(m):
        for i in range(1, DP):
            blk = qs.at[m, i]
            rcopy(blk, blk, q_ssem.at[m, i], q_rsem.at[m, i], peer(1, 0)).wait_send()

    def m_copy(m, i, k):
        return rcopy(msend.at[m, i, k], mrecv.at[m, i, k], m_ssem.at[m, i, k], m_rsem.at[m, i, k], (s, d, t1))

    def a_copy(m, k):
        return rcopy(asend.at[m, k], abuf.at[m, k], ab_ssem.at[0, m, k], a_rsem.at[m, k], (sp, d, t))

    def b_copy(m, k):
        return rcopy(bsend.at[m, k], bbuf.at[m, k], ab_ssem.at[1, m, k], b_rsem.at[m, k], (sp, d, t2))

    def f_copy(m, k):
        return rcopy(bsend.at[m, k], bfin.at[m, k], ab_ssem.at[1, m, k], f_rsem.at[m, k], (s, d, t2))

    def l_copy(m, k):
        return rcopy(dyb.at[m, k], lig.at[m, k], l_ssem.at[m, k], l_rsem.at[m, k], (sn, d, t))

    def early_hop():
        @pl.when(s == 0)
        def _():
            q_hop(0)

    def backward(m):
        key = qkv[m, :, QC : QC + HD]
        val = qkv[m, :, QC + HD :]
        inv = invb[m, :, 0:1]
        dk = jnp.zeros((L, HD), F32)
        dv = jnp.zeros((L, HD), F32)
        rd = jnp.zeros((L, 1), F32)
        for k in range(2):
            @pl.when(s < SECTIONS - 1)
            def _():
                a_copy(m, k).wait_recv()
                b_copy(m, k).wait_recv()
                dyb[m, k] = (abuf[m, k].astype(F32) + bbuf[m, k].astype(F32)).astype(BF)
                l_copy(m, k).start()

            do = stack_heads(dyb[m, k])
            q = stack_heads(qkv[m, :, k * HB : (k + 1) * HB])
            pr = probs[m, k]
            dp = dot(do, val, NT)
            ds = pr * (dp - jnp.sum(dp * pr, axis=1, keepdims=True))
            dsb = ds.astype(BF)
            dq = (dot(dsb, key) * SCALE).astype(BF)
            dqkv[m, :, k * HB : (k + 1) * HB] = unstack_heads(dq)
            fold = (ds[:, :W] + ds[:, W:]).astype(BF)
            for h in range(4):
                qown[m, k, :L, h * W : (h + 1) * W] = fold[h * L : (h + 1) * L]
            dk += dot(dsb, q, TN)
            dv += dot(pr.astype(BF), do, TN)
            qd = jnp.sum(q.astype(F32) * dq.astype(F32), axis=1, keepdims=True)
            for i in range(4):
                rd += qd[i * L : (i + 1) * L]
        dkb = (dk * SCALE).astype(BF)
        dvb = dv.astype(BF)
        dqkv[m, :, QC : QC + HD] = dkb
        dqkv[m, :, QC + HD :] = dvb
        qown[m, 0, L:, :] = dkb
        qown[m, 1, L:, :] = dvb
        rd += jnp.sum(
            key.astype(F32) * dkb.astype(F32) + val.astype(F32) * dvb.astype(F32), axis=1, keepdims=True
        )
        q_start(m)
        if m == 1:
            early_hop()
        coef = inv * inv * rd / D
        grads = dqkv[m]

        def term(j, k):
            part = dot(grads, w[pl.ds(pl.multiple_of(j * BLK + k * HB, HB), HB), :], NT)
            return inv * gains(j, k) * part - hbuf[m, j, k].astype(F32) * coef

        for k in range(2):
            for i, j in enumerate((t3, t1)):
                msend[m, i, k] = term(j, k).astype(BF)
                m_copy(m, i, k).start()
        for k in range(2):
            own = term(t2, k)
            m_copy(m, 0, k).wait_recv()
            bsend[m, k] = (own + mrecv[m, 0, k].astype(F32)).astype(BF)

            @pl.when(s > 0)
            def _():
                b_copy(m, k).start()

            @pl.when(s == 0)
            def _():
                f_copy(m, k).start()

            own = term(t, k) + dyb[m, k].astype(F32)
            m_copy(m, 1, k).wait_recv()
            asend[m, k] = (own + mrecv[m, 1, k].astype(F32)).astype(BF)

            @pl.when(s > 0)
            def _():
                a_copy(m, k).start()

    for m in range(MB):
        forward(m)

    @pl.when(s < SECTIONS - 1)
    def _():
        for m in range(MB):
            send_rows(m)

    @pl.when(s < 2)
    def _():
        for m in range(MB):
            u_pass(m)

    backward(0)
    backward(1)

    @pl.when(s == SECTIONS - 1)
    def _():
        for m in range(MB):
            send_rows(m)

    @pl.when(s > 0)
    def _():
        q_hop(0)

    @pl.when(s >= 2)
    def _():
        for m in range(MB):
            u_pass(m)

    def u_wait(m):
        for rz in range(8):
            u_wait_one(m, place(rz, 1))

    def weight_grads(m, lo, hi, block, i):
        u = uall[m, lo:hi, 2 * block + i].reshape((hi - lo) * L, HD)
        g = dqall[m, lo:hi].reshape((hi - lo) * L, HB + HD)
        part = dot(u, g, TN)
        if m == 0 and lo == 0:
            gtot[block, i] = part
        else:
            gtot[block, i] += part

    u_wait(0)
    q_near(0)
    q_make(0, 0, 10)
    q_hop(1)
    u_wait(1)
    q_far(0)
    q_make(0, 10, DP)
    q_near(1)
    q_make(1, 0, 10)
    for block in range(2):
        for i in range(2):
            weight_grads(0, 0, DP, block, i)
            weight_grads(1, 0, 10, block, i)

    @pl.when(s == 0)
    def _():
        for m in range(MB):
            for k in range(2):
                f_copy(m, k).wait_recv()
                lig[m, k] = (asend[m, k].astype(F32) + bfin[m, k].astype(F32)).astype(BF)

    @pl.when(s > 0)
    def _():
        for m in range(MB):
            for k in range(2):
                l_copy(m, k).wait_recv()

    for m in range(MB):
        for k in range(2):
            o_lig[0, 0, m, :, k * HB : (k + 1) * HB] = lig[m, k]

    q_far(1)
    q_make(1, 10, DP)

    def x_copy(i):
        return rcopy(xsend.at[i], xrecv.at[i], x_ssem.at[i], x_rsem.at[i], peer(0, 1))

    for i in range(2):
        weight_grads(1, 10, DP, 1 - xl, i)
        xsend[i] = gtot[1 - xl, i].astype(BF)
        x_copy(i).start()
    for i in range(2):
        weight_grads(1, 10, DP, xl, i)

    eye = lax.broadcasted_iota(jnp.int32, (HD, HD), 0) == lax.broadcasted_iota(jnp.int32, (HD, HD), 1)
    for block in range(2):
        for i in range(2):
            rows = pl.ds(pl.multiple_of((2 * z + block) * ROWS + i * HD, HD), HD)
            wide = w[rows, pl.ds(pl.multiple_of(xl * HB, HB), HB)].astype(F32)
            narrow = w[rows, pl.ds(pl.multiple_of(QC + xl * HD, HD), HD)].astype(F32)
            total = gtot[block, i]
            col = jnp.sum(total[:, :HB] * wide, axis=1, keepdims=True) + jnp.sum(
                total[:, HB:] * narrow, axis=1, keepdims=True
            )
            row = jnp.sum(jnp.where(eye, jnp.broadcast_to(col, (HD, HD)), 0.0), axis=0, keepdims=True)
            ggsend[block, :, i * HD : (i + 1) * HD] = jnp.broadcast_to(row, (8, HD))

    def gg_copy(block, j):
        n = 4 * block + j
        src = 2 * t + xl
        return rcopy(
            ggsend.at[block], ggrecv.at[src], gg_ssem.at[n], gg_rsem.at[src], (s, 8 * lax.rem(z, 2) + n, z // 2)
        )

    for block in range(2):
        for j in range(4):
            mine = loop & (lax.rem(d, 8) == 4 * block + j)

            @pl.when(jnp.logical_not(mine))
            def _():
                gg_copy(block, j).start()

            @pl.when(mine)
            def _():
                ggrecv[2 * t + xl] = ggsend[block]

    for i in range(2):
        x_copy(i).wait_recv()
        grow = g16[d, 0:1, i * HD : (i + 1) * HD]
        gcol = jnp.sum(jnp.where(eye, jnp.broadcast_to(grow, (HD, HD)), 0.0), axis=1, keepdims=True)
        own = gtot[xl, i]
        other = xrecv[i].astype(F32)
        first = jnp.where(xl == 0, own, other) * gcol
        second = jnp.where(xl == 0, other, own) * gcol
        rs = slice(i * HD, (i + 1) * HD)
        o_gq[0, rs, :HB] = first[:, :HB]
        o_gq[0, rs, HB:] = second[:, :HB]
        o_gkv[0, rs, :HD] = first[:, HB:]
        o_gkv[0, rs, HD:] = second[:, HB:]

    gsum = jnp.zeros((8, ROWS), F32)
    for i in range(8):
        @pl.when(jnp.logical_not(loop & (t == i // 2) & (xl == i % 2)))
        def _():
            rcopy(
                ggsend.at[0], ggrecv.at[i], gg_ssem.at[0], gg_rsem.at[i], (s, 2 * zs + i % 2, i // 2)
            ).wait_recv()
        gsum += ggrecv[i]
    quarter = lax.rem(d, 4)
    picked = jnp.zeros((1, L), F32)
    for j in range(4):
        picked += jnp.where(quarter == j, 1.0, 0.0) * gsum[0:1, j * L : (j + 1) * L]
    o_gg[...] = picked

    for i, tt in enumerate((t1, t2, t3)):
        g_copy(i, tt).wait_send()
    for m in range(MB):
        for k in range(2):
            h_copy(m, k, 2, t, hbuf.at[m, t, k], (s, d, t1)).wait_send()
            h_copy(m, k, 3, t2, hbuf.at[m, t2, k], (s, d, t1)).wait_send()

            @pl.when(s == 0)
            def _():
                h_copy(m, k, 4, t, hbuf.at[m, t, k], (s, d, t2)).wait_send()

            @pl.when(s < SECTIONS - 1)
            def _():
                h_copy(m, k, 0, t, outb.at[m, k], (sn, d, t)).wait_send()
                h_copy(m, k, 1, t, outb.at[m, k], (sn, d, t2)).wait_send()
                l_copy(m, k).wait_send()

            for i in range(2):
                m_copy(m, i, k).wait_send()
            b_copy(m, k).wait_send()

            @pl.when(s > 0)
            def _():
                a_copy(m, k).wait_send()

        for rz in range(8):
            u_copy(m, rz).wait_send()
            if rz:
                u_pass_copy(m, rz).wait_send()
        q_drain(m)
    for i in range(2):
        x_copy(i).wait_send()
    for block in range(2):
        for j in range(4):
            @pl.when(jnp.logical_not(loop & (lax.rem(d, 8) == 4 * block + j)))
            def _():
                gg_copy(block, j).wait_send()


def hand_out(*refs):
    for i in range(4):
        refs[4 + i][...] = refs[i][...]


def body(hidden_in, teacher, segment_ids, w_query, w_keyval, norm_gain):
    vmem = pl.BlockSpec(memory_space=pltpu.VMEM)
    hbm = pl.BlockSpec(memory_space=pl.ANY)
    dma = pltpu.SemaphoreType.DMA
    V = pltpu.VMEM
    out = pl.pallas_call(
        kernel,
        out_shape=(
            jax.ShapeDtypeStruct((1, ROWS, QC), F32),
            jax.ShapeDtypeStruct((1, ROWS, KC), F32),
            jax.ShapeDtypeStruct((1, L), F32),
            jax.ShapeDtypeStruct((1, 1, MB, L, BLK), BF),
        ),
        in_specs=[vmem, vmem, vmem, hbm, hbm, vmem],
        out_specs=(vmem, vmem, vmem, vmem),
        scratch_shapes=[
            V((D, C), BF),
            V((MB, TENSOR, 2, L, HB), BF),
            V((DP, 8, ROWS), F32),
            V((L, C), F32),
            V((MB, L, C), BF),
            V((MB, 2, 4 * L, L), F32),
            V((MB, L, L), F32),
            V((MB, L, 128), F32),
            V((MB, 2, L, HB), BF),
            V((MB, 2, L, HB), BF),
            V((MB, 8, 5, L, HD), BF),
            V((MB, DP, 5, L, HD), BF),
            V((MB, 2, 2 * L, HD), BF),
            V((MB, DP, 2 * L, HD), BF),
            V((2, L, HD), BF),
            V((2, 2 * HD, HB), BF),
            V((MB, L, C), BF),
            V((MB, DP, L, HB + HD), BF),
            V((MB, 2, 2, L, HB), BF),
            V((MB, 2, 2, L, HB), BF),
            V((MB, 2, L, HB), BF),
            V((MB, 2, L, HB), BF),
            V((MB, 2, L, HB), BF),
            V((MB, 2, L, HB), BF),
            V((MB, 2, L, HB), BF),
            V((MB, 2, L, HB), BF),
            V((2, 2, HD, HB + HD), F32),
            V((2, HD, HB + HD), BF),
            V((2, HD, HB + HD), BF),
            V((2, 8, ROWS), F32),
            V((8, 8, ROWS), F32),
            dma((2, TENSOR)),
            dma((3,)),
            dma((TENSOR,)),
            dma((MB, 5, 2)),
            dma((MB, TENSOR, 2)),
            dma((MB, DP)),
            dma((MB, DP)),
            dma((MB, DP)),
            dma((MB, DP)),
            dma((MB, 2, 2)),
            dma((MB, 2, 2)),
            dma((2, MB, 2)),
            dma((MB, 2)),
            dma((MB, 2)),
            dma((MB, 2)),
            dma((MB, 2)),
            dma((MB, 2)),
            dma((8,)),
            dma((8,)),
            dma((2,)),
            dma((2,)),
        ],
        compiler_params=pltpu.CompilerParams(
            collective_id=1, has_side_effects=True, vmem_limit_bytes=58 * 1024 * 1024
        ),
        name="train_step",
    )(hidden_in, teacher, segment_ids, w_query, w_keyval, norm_gain)
    return pl.pallas_call(
        hand_out,
        out_shape=tuple(jax.ShapeDtypeStruct(o.shape, o.dtype) for o in out),
        in_specs=[vmem] * 4,
        out_specs=(vmem,) * 4,
        name="hand_out",
    )(*out)


def solution(mesh):
    in_specs = (
        P("dp", None, None, "tensor"),
        P("dp", None, None, "tensor"),
        P("dp", None, None),
        P("section", None, "tensor"),
        P("section", None, "tensor"),
        P("section", "tensor"),
    )
    out_specs = (
        P("section", "dp", "tensor"),
        P("section", "dp", "tensor"),
        P("section", ("tensor", "dp")),
        P("section", "dp", None, None, "tensor"),
    )
    return jax.shard_map(body, mesh=mesh, in_specs=in_specs, out_specs=out_specs, check_vma=False)
```

```python
import math

import jax
import jax.numpy as jnp
from jax import lax
from jax.experimental import pallas as pl
from jax.experimental.pallas import tpu as pltpu
from jax.sharding import PartitionSpec as P

EPSILON = 1e-05
D = 4096
HD = 128
L = 64
W = 32
MB = 2
DP = 16
SECTIONS = 4
TENSOR = 4
ROWS = D // DP
QC = 1024
KC = 256
C = QC + KC
BLK = 1024
HB = BLK // 2
BF = jnp.bfloat16
F32 = jnp.float32
MESH = pl.DeviceIdType.MESH
SCALE = 1.0 / math.sqrt(HD)
NT = (((1,), (1,)), ((), ()))
TN = (((0,), (0,)), ((), ()))
NN = (((1,), (0,)), ((), ()))


def dot(a, b, dims=NN):
    return lax.dot_general(a, b, dims, preferred_element_type=F32)


def place(rz, c):
    rz = rz % 8
    near = 0 if rz == 0 else 2 * rz - 1 if rz <= 4 else 2 * (8 - rz)
    return 2 * near + c


def stack_heads(x):
    return jnp.concatenate([x[:, i * HD : (i + 1) * HD] for i in range(x.shape[1] // HD)], axis=0)


def unstack_heads(x):
    return jnp.concatenate([x[i * L : (i + 1) * L] for i in range(x.shape[0] // L)], axis=1)


def kernel(
    hid, tea, seg, wq, wkv, gain,
    o_gq, o_gkv, o_gg, o_lig,
    w, hbuf, g16, acc, qkv, probs, mask, invb, pown, pbuf, dyb,
    usend, uall, qown, qs, low, kdiag, dqkv, dqall, msend, mrecv, bsend, asend, abuf, bbuf, bfin, lig, gtot, xsend, xrecv, ggsend, ggrecv,
    w_sem, g_ssem, g_rsem, h_ssem, h_rsem, p_ssem, p_rsem, u_ssem, u_rsem, q_ssem, q_rsem,
    m_ssem, m_rsem, ab_ssem, a_rsem, b_rsem, f_rsem, l_ssem, l_rsem, gg_ssem, gg_rsem, x_ssem, x_rsem,
):
    s = lax.axis_index("section")
    d = lax.axis_index("dp")
    t = lax.axis_index("tensor")
    t1 = t + 1 - 2 * lax.rem(t, 2)
    t2 = lax.rem(t + 2, 4)
    t3 = 3 - t
    z = d // 2
    xl = lax.rem(d, 2)
    sn = lax.rem(s + 1, SECTIONS)
    sp = lax.rem(s + SECTIONS - 1, SECTIONS)

    def rcopy(src, dst, ssem, rsem, dev):
        return pltpu.make_async_remote_copy(
            src_ref=src, dst_ref=dst, send_sem=ssem, recv_sem=rsem, device_id=dev, device_id_type=MESH
        )

    bar = pltpu.get_barrier_semaphore()
    for dev in ((s, d, t1), (s, d, t2), (s, d, t3), (sn, d, t), (sn, d, t2), (sp, d, t), (sp, d, t2)):
        pl.semaphore_signal(bar, inc=1, device_id=dev, device_id_type=MESH)

    def greet(i, _):
        pl.semaphore_signal(bar, inc=1, device_id=(s, lax.rem(d + i, DP), t), device_id_type=MESH)
        return 0

    lax.fori_loop(1, DP, greet, 0)
    loop = (t == z // 2) & (z // 4 == lax.rem(z, 2))
    zs = 2 * t + d // 8
    for i in range(8):
        @pl.when(jnp.logical_not(loop & (t == i // 2) & (xl == i % 2)))
        def _():
            pl.semaphore_signal(bar, inc=1, device_id=(s, 2 * zs + i % 2, i // 2), device_id_type=MESH)

    def w_copies(j):
        rows = pl.ds(pl.multiple_of(j * BLK, BLK), BLK)
        return (
            pltpu.make_async_copy(wq.at[0, rows, :], w.at[rows, pl.ds(0, QC)], w_sem.at[0, j]),
            pltpu.make_async_copy(wkv.at[0, rows, :], w.at[rows, pl.ds(QC, KC)], w_sem.at[1, j]),
        )

    for j in (t, t2, t1, t3):
        for c in w_copies(j):
            c.start()

    ri = lax.broadcasted_iota(jnp.int32, (L, L), 0)
    ci = lax.broadcasted_iota(jnp.int32, (L, L), 1)
    for m in range(MB):
        srow = jnp.broadcast_to(seg[0, m : m + 1, :], (L, L))
        scol = jnp.sum(jnp.where(ri == ci, srow, 0), axis=1, keepdims=True)
        mask[m] = jnp.where((srow == scol) & (ri >= ci), 1.0, 0.0)
    fi = lax.broadcasted_iota(jnp.int32, (L, HD), 0)
    fj = lax.rem(lax.broadcasted_iota(jnp.int32, (L, HD), 1), W)
    low[0] = jnp.where(fj > fi - W, 1.0, 0.0).astype(BF)
    low[1] = jnp.where(fj > fi - W, 0.0, 1.0).astype(BF)
    kdiag[...] = jnp.zeros_like(kdiag)
    for i in range(4):
        g16[4 * t + i] = jnp.broadcast_to(gain[:, i * ROWS : (i + 1) * ROWS].astype(F32), (8, ROWS))

    pl.semaphore_wait(bar, 30 - jnp.where(loop, 1, 0))

    def g_copy(i, dev_t):
        sl = g16.at[pl.ds(4 * t, 4)]
        return rcopy(sl, sl, g_ssem.at[i], g_rsem.at[t], (s, d, dev_t))

    def hid_copy(m, k, kind):
        slot = t2 if kind == 2 else t
        src = hbuf.at[m, slot, k] if kind == 2 else hid.at[0, m, :, pl.ds(k * HB, HB)]
        return rcopy(
            src, hbuf.at[m, slot, k], h_ssem.at[m, kind, k], h_rsem.at[m, slot, k], (s, d, t1 if kind else t2)
        )

    def h_wait(m, slot, k):
        blk = hbuf.at[m, slot, k]
        rcopy(blk, blk, h_ssem.at[m, 0, k], h_rsem.at[m, slot, k], (s, d, t1)).wait_recv()

    def p_copy(m, src, layer, slot, kind):
        dev = ((sn, d, t), (sn, d, t2), (s, d, t1), (s, d, t1))[kind]
        return rcopy(
            src, pbuf.at[m, layer, slot], p_ssem.at[m, layer, kind], p_rsem.at[m, layer, slot], dev
        )

    def p_wait(m, layer, slot):
        p_copy(m, pbuf.at[m, layer, slot], layer, slot, 2).wait_recv()

    for i, tt in enumerate((t1, t2, t3)):
        g_copy(i, tt).start()

    for m in range(MB):
        for k in range(2):
            hid_copy(m, k, 0).start()
            hid_copy(m, k, 1).start()
            hbuf[m, t, k] = hid[0, m, :, k * HB : (k + 1) * HB]

    for tt in (t1, t2, t3):
        sl = g16.at[pl.ds(4 * tt, 4)]
        rcopy(sl, sl, g_ssem.at[0], g_rsem.at[tt], (s, d, tt)).wait_recv()

    def gains(j, k):
        p = 4 * j + 2 * k
        return jnp.concatenate([g16[p, 0:1, :], g16[p + 1, 0:1, :]], axis=1)

    def forward(m):
        ss = jnp.zeros((L, 1), F32)

        def kstep(j, k, first):
            x = hbuf[m, j, k].astype(F32)
            part_ss = jnp.sum(x * x, axis=1, keepdims=True)
            xg = (x * gains(j, k)).astype(BF)
            part = dot(xg, w[pl.ds(pl.multiple_of(j * BLK + k * HB, HB), HB), :])
            if first:
                acc[...] = part
            else:
                acc[...] += part
            return part_ss

        def need_w(j):
            if m == 0:
                for c in w_copies(j):
                    c.wait()

        def rebuild(layer, j, b):
            vd = kdiag.at[b]
            for h in range(4):
                vd[h * W : (h + 1) * W, h * HD : (h + 1) * HD] = pbuf[m, layer, j, 2, :W]
                vd[HD + h * W : HD + (h + 1) * W, h * HD : (h + 1) * HD] = pbuf[m, layer, j, 2, W:]
            for k in range(2):
                fold = pbuf[m, layer, j, k]
                both = jnp.concatenate([fold * low[0], fold * low[1]], axis=1)
                o = dot(both, vd[...]).astype(BF)
                hbuf[m, j, k] = (hbuf[m, j, k].astype(F32) + o.astype(F32)).astype(BF)

        for k in range(2):
            h_wait(m, t2, k)
            hid_copy(m, k, 2).start()

        @pl.when(s > 0)
        def _():
            for k in range(2):
                hid_copy(m, k, 2).wait_send()

        for layer in range(SECTIONS - 1):
            @pl.when(s > layer)
            def _():
                mine = pbuf.at[m, layer, t]
                p_wait(m, layer, t)
                p_copy(m, mine, layer, t, 2).start()

                @pl.when(s < SECTIONS - 1)
                def _():
                    p_copy(m, mine, layer, t, 1).start()
                    p_copy(m, mine, layer, t, 0).start()

                p_wait(m, layer, t2)
                p_copy(m, pbuf.at[m, layer, t2], layer, t2, 3).start()
                rebuild(layer, t, 0)
                rebuild(layer, t2, 1)

        need_w(t)
        ss += kstep(t, 0, True)
        ss += kstep(t, 1, False)
        need_w(t2)
        ss += kstep(t2, 0, False)
        ss += kstep(t2, 1, False)
        for j in (t1, t3):
            for k in range(2):
                h_wait(m, j, k)
        for layer in range(SECTIONS - 1):
            @pl.when(s > layer)
            def _():
                p_wait(m, layer, t1)
                rebuild(layer, t1, 0)
                p_wait(m, layer, t3)
                rebuild(layer, t3, 1)

        for j in (t1, t3):
            need_w(j)
            ss += kstep(j, 0, False)
            ss += kstep(j, 1, False)
        inv = lax.rsqrt(ss / D + EPSILON)
        invb[m] = jnp.broadcast_to(inv, (L, 128))
        qkv[m] = (acc[...] * inv).astype(BF)
        key = qkv[m, :, QC : QC + HD]
        val = qkv[m, :, QC + HD :]
        allowed = jnp.concatenate([mask[m]] * 4, axis=0) > 0.0
        for k in range(2):
            q = stack_heads(qkv[m, :, k * HB : (k + 1) * HB])
            sc = dot(q, key, NT) * SCALE
            e = jnp.exp(jnp.where(allowed, sc, -1e30))
            pr = e / jnp.sum(e, axis=1, keepdims=True)
            probs[m, k] = pr
            fold = (pr[:, :W] + pr[:, W:]).astype(BF)
            for h in range(4):
                pown[m, k, :, h * W : (h + 1) * W] = fold[h * L : (h + 1) * L]

            @pl.when(s == SECTIONS - 1)
            def _():
                o = unstack_heads(dot(pr.astype(BF), val).astype(BF)).astype(F32)
                hn = (hbuf[m, t, k].astype(F32) + o).astype(BF)
                dyb[m, k] = (
                    hn.astype(F32) - tea[0, m, :, k * HB : (k + 1) * HB].astype(F32)
                ).astype(BF)

        pown[m, 2] = val

        @pl.when(s < SECTIONS - 1)
        def _():
            p_copy(m, pown.at[m], s, t, 1).start()
            p_copy(m, pown.at[m], s, t, 0).start()

    def peer(rz, c):
        return (s, 2 * lax.rem(z + rz % 8, 8) + (1 - xl if c else xl), t)

    def u_copy(m, rz):
        slot = place(-rz, 0) if rz else place(0, 1)
        src = usend.at[m, lax.rem(z + rz, 8) if rz else z]
        return rcopy(src, uall.at[m, slot], u_ssem.at[m, slot], u_rsem.at[m, slot], peer(rz, 0 if rz else 1))

    def u_pass_copy(m, rz):
        slot = place(rz, 1)
        return rcopy(
            uall.at[m, place(rz, 0)], uall.at[m, slot], u_ssem.at[m, slot], u_rsem.at[m, slot], peer(0, 1)
        )

    def u_pass(m):
        for rz in (1, 7, 2, 6, 3, 5, 4):
            u_wait_one(m, place(rz, 0))
            u_pass_copy(m, rz).start()

    def u_wait_one(m, i):
        blk = uall.at[m, i]
        rcopy(blk, blk, u_ssem.at[m, i], u_rsem.at[m, i], peer(1, 0)).wait_recv()

    def send_rows(m):
        inv = invb[m, :, 0:1]
        for j in range(TENSOR):
            for k in range(2):
                u = (hbuf[m, j, k].astype(F32) * inv).astype(BF)
                for i in range(4):
                    usend[m, 2 * j + k, i] = u[:, i * HD : (i + 1) * HD]
        for p in range(8):
            usend[m, p, 4] = qkv[m, :, QC : QC + HD]
        uall[m, 0] = usend[m, z]
        for rz in (0, 1, 7, 2, 6, 3, 5, 4):
            u_copy(m, rz).start()


    def q_copy(m, src, rz, c, step, dc):
        dst = place(rz - step, c ^ dc)
        return rcopy(src, qs.at[m, dst], q_ssem.at[m, dst], q_rsem.at[m, dst], peer(step, dc))

    def q_wait(m, rz, c):
        blk = qs.at[m, place(rz, c)]
        rcopy(blk, blk, q_ssem.at[m, 0], q_rsem.at[m, place(rz, c)], peer(1, 0)).wait_recv()

    def q_start(m):
        qs[m, 0] = qown[m, xl]
        for step in (2, 6, 1, 7, 0):
            for c in range(2):
                if step or c:
                    q_copy(m, qown.at[m, 1 - xl if c else xl], 0, 0, step, c).start()

    def q_hop(m):
        for c in range(2):
            for sg in (1, -1):
                q_wait(m, -2 * sg, c)
                src = qs.at[m, place(-2 * sg, c)]
                q_copy(m, src, -2 * sg, c, sg, 0).start()
                if c == (0 if sg == 1 else 1):
                    q_copy(m, src, -2 * sg, c, 2 * sg, 0).start()

    def q_near(m):
        for rz, c in ((0, 1), (1, 0), (-1, 0), (1, 1), (-1, 1)):
            q_wait(m, rz, c)

    def q_far(m):
        for rz in (3, -3, 4):
            for c in range(2):
                q_wait(m, rz, c)

    def q_make(m, lo, hi):
        for i in range(lo, hi):
            pair = kdiag.at[i % 2]
            for h in range(4):
                pair[h * W : (h + 1) * W, h * HD : (h + 1) * HD] = uall[m, i, 4, :W]
                pair[HD + h * W : HD + (h + 1) * W, h * HD : (h + 1) * HD] = uall[m, i, 4, W:]
            fold = qs[m, i, :L, :]
            both = jnp.concatenate([fold * low[0], fold * low[1]], axis=1)
            dqall[m, i, :, :HB] = (dot(both, pair[...]) * SCALE).astype(BF)
            dqall[m, i, :, HB:] = qs[m, i, L:, :]

    def q_drain(m):
        for i in range(1, DP):
            blk = qs.at[m, i]
            rcopy(blk, blk, q_ssem.at[m, i], q_rsem.at[m, i], peer(1, 0)).wait_send()

    def m_copy(m, i, k):
        return rcopy(msend.at[m, i, k], mrecv.at[m, i, k], m_ssem.at[m, i, k], m_rsem.at[m, i, k], (s, d, t1))

    def a_copy(m, k):
        return rcopy(asend.at[m, k], abuf.at[m, k], ab_ssem.at[0, m, k], a_rsem.at[m, k], (sp, d, t))

    def b_copy(m, k):
        return rcopy(bsend.at[m, k], bbuf.at[m, k], ab_ssem.at[1, m, k], b_rsem.at[m, k], (sp, d, t2))

    def f_copy(m, k):
        return rcopy(bsend.at[m, k], bfin.at[m, k], ab_ssem.at[1, m, k], f_rsem.at[m, k], (s, d, t2))

    def l_copy(m, k):
        return rcopy(dyb.at[m, k], lig.at[m, k], l_ssem.at[m, k], l_rsem.at[m, k], (sn, d, t))

    def early_hop():
        @pl.when(s == 0)
        def _():
            q_hop(0)

    def backward(m):
        key = qkv[m, :, QC : QC + HD]
        val = qkv[m, :, QC + HD :]
        inv = invb[m, :, 0:1]
        dk = jnp.zeros((L, HD), F32)
        dv = jnp.zeros((L, HD), F32)
        rd = jnp.zeros((L, 1), F32)
        for k in range(2):
            @pl.when(s < SECTIONS - 1)
            def _():
                a_copy(m, k).wait_recv()
                b_copy(m, k).wait_recv()
                dyb[m, k] = (abuf[m, k].astype(F32) + bbuf[m, k].astype(F32)).astype(BF)
                l_copy(m, k).start()

            do = stack_heads(dyb[m, k])
            q = stack_heads(qkv[m, :, k * HB : (k + 1) * HB])
            pr = probs[m, k]
            dp = dot(do, val, NT)
            ds = pr * (dp - jnp.sum(dp * pr, axis=1, keepdims=True))
            dsb = ds.astype(BF)
            dq = (dot(dsb, key) * SCALE).astype(BF)
            dqkv[m, :, k * HB : (k + 1) * HB] = unstack_heads(dq)
            fold = (ds[:, :W] + ds[:, W:]).astype(BF)
            for h in range(4):
                qown[m, k, :L, h * W : (h + 1) * W] = fold[h * L : (h + 1) * L]
            dk += dot(dsb, q, TN)
            dv += dot(pr.astype(BF), do, TN)
            qd = jnp.sum(q.astype(F32) * dq.astype(F32), axis=1, keepdims=True)
            for i in range(4):
                rd += qd[i * L : (i + 1) * L]
        dkb = (dk * SCALE).astype(BF)
        dvb = dv.astype(BF)
        dqkv[m, :, QC : QC + HD] = dkb
        dqkv[m, :, QC + HD :] = dvb
        qown[m, 0, L:, :] = dkb
        qown[m, 1, L:, :] = dvb
        rd += jnp.sum(
            key.astype(F32) * dkb.astype(F32) + val.astype(F32) * dvb.astype(F32), axis=1, keepdims=True
        )
        q_start(m)
        if m == 1:
            early_hop()
        coef = inv * inv * rd / D
        grads = dqkv[m]

        def term(j, k):
            part = dot(grads, w[pl.ds(pl.multiple_of(j * BLK + k * HB, HB), HB), :], NT)
            return inv * gains(j, k) * part - hbuf[m, j, k].astype(F32) * coef

        for k in range(2):
            for i, j in enumerate((t3, t1)):
                msend[m, i, k] = term(j, k).astype(BF)
                m_copy(m, i, k).start()
        for k in range(2):
            own = term(t2, k)
            m_copy(m, 0, k).wait_recv()
            bsend[m, k] = (own + mrecv[m, 0, k].astype(F32)).astype(BF)

            @pl.when(s > 0)
            def _():
                b_copy(m, k).start()

            @pl.when(s == 0)
            def _():
                f_copy(m, k).start()

            own = term(t, k) + dyb[m, k].astype(F32)
            m_copy(m, 1, k).wait_recv()
            asend[m, k] = (own + mrecv[m, 1, k].astype(F32)).astype(BF)

            @pl.when(s > 0)
            def _():
                a_copy(m, k).start()

    for m in range(MB):
        forward(m)

    @pl.when(s < SECTIONS - 1)
    def _():
        for m in range(MB):
            send_rows(m)

    @pl.when(s < 2)
    def _():
        for m in range(MB):
            u_pass(m)

    backward(0)
    backward(1)

    @pl.when(s == SECTIONS - 1)
    def _():
        for m in range(MB):
            send_rows(m)

    @pl.when(s > 0)
    def _():
        q_hop(0)

    @pl.when(s >= 2)
    def _():
        for m in range(MB):
            u_pass(m)

    def u_wait(m):
        for rz in range(8):
            u_wait_one(m, place(rz, 1))

    def weight_grads(m, lo, hi, block, i):
        u = uall[m, lo:hi, 2 * block + i].reshape((hi - lo) * L, HD)
        g = dqall[m, lo:hi].reshape((hi - lo) * L, HB + HD)
        part = dot(u, g, TN)
        if m == 0 and lo == 0:
            gtot[block, i] = part
        else:
            gtot[block, i] += part

    u_wait(0)
    q_near(0)
    q_make(0, 0, 10)
    q_hop(1)
    u_wait(1)
    q_far(0)
    q_make(0, 10, DP)
    q_near(1)
    q_make(1, 0, 10)
    for block in range(2):
        for i in range(2):
            weight_grads(0, 0, DP, block, i)
            weight_grads(1, 0, 10, block, i)

    @pl.when(s == 0)
    def _():
        for m in range(MB):
            for k in range(2):
                f_copy(m, k).wait_recv()
                lig[m, k] = (asend[m, k].astype(F32) + bfin[m, k].astype(F32)).astype(BF)

    @pl.when(s > 0)
    def _():
        for m in range(MB):
            for k in range(2):
                l_copy(m, k).wait_recv()

    for m in range(MB):
        for k in range(2):
            o_lig[0, 0, m, :, k * HB : (k + 1) * HB] = lig[m, k]

    q_far(1)
    q_make(1, 10, DP)

    def x_copy(i):
        return rcopy(xsend.at[i], xrecv.at[i], x_ssem.at[i], x_rsem.at[i], peer(0, 1))

    for i in range(2):
        weight_grads(1, 10, DP, 1 - xl, i)
        xsend[i] = gtot[1 - xl, i].astype(BF)
        x_copy(i).start()
    for i in range(2):
        weight_grads(1, 10, DP, xl, i)

    eye = lax.broadcasted_iota(jnp.int32, (HD, HD), 0) == lax.broadcasted_iota(jnp.int32, (HD, HD), 1)
    for block in range(2):
        for i in range(2):
            rows = pl.ds(pl.multiple_of((2 * z + block) * ROWS + i * HD, HD), HD)
            wide = w[rows, pl.ds(pl.multiple_of(xl * HB, HB), HB)].astype(F32)
            narrow = w[rows, pl.ds(pl.multiple_of(QC + xl * HD, HD), HD)].astype(F32)
            total = gtot[block, i]
            col = jnp.sum(total[:, :HB] * wide, axis=1, keepdims=True) + jnp.sum(
                total[:, HB:] * narrow, axis=1, keepdims=True
            )
            row = jnp.sum(jnp.where(eye, jnp.broadcast_to(col, (HD, HD)), 0.0), axis=0, keepdims=True)
            ggsend[block, :, i * HD : (i + 1) * HD] = jnp.broadcast_to(row, (8, HD))

    def gg_copy(block, j):
        n = 4 * block + j
        src = 2 * t + xl
        return rcopy(
            ggsend.at[block], ggrecv.at[src], gg_ssem.at[n], gg_rsem.at[src], (s, 8 * lax.rem(z, 2) + n, z // 2)
        )

    for block in range(2):
        for j in range(4):
            mine = loop & (lax.rem(d, 8) == 4 * block + j)

            @pl.when(jnp.logical_not(mine))
            def _():
                gg_copy(block, j).start()

            @pl.when(mine)
            def _():
                ggrecv[2 * t + xl] = ggsend[block]

    for i in range(2):
        x_copy(i).wait_recv()
        grow = g16[d, 0:1, i * HD : (i + 1) * HD]
        gcol = jnp.sum(jnp.where(eye, jnp.broadcast_to(grow, (HD, HD)), 0.0), axis=1, keepdims=True)
        own = gtot[xl, i]
        other = xrecv[i].astype(F32)
        first = jnp.where(xl == 0, own, other) * gcol
        second = jnp.where(xl == 0, other, own) * gcol
        rs = slice(i * HD, (i + 1) * HD)
        o_gq[0, rs, :HB] = first[:, :HB]
        o_gq[0, rs, HB:] = second[:, :HB]
        o_gkv[0, rs, :HD] = first[:, HB:]
        o_gkv[0, rs, HD:] = second[:, HB:]

    gsum = jnp.zeros((8, ROWS), F32)
    for i in range(8):
        @pl.when(jnp.logical_not(loop & (t == i // 2) & (xl == i % 2)))
        def _():
            rcopy(
                ggsend.at[0], ggrecv.at[i], gg_ssem.at[0], gg_rsem.at[i], (s, 2 * zs + i % 2, i // 2)
            ).wait_recv()
        gsum += ggrecv[i]
    quarter = lax.rem(d, 4)
    picked = jnp.zeros((1, L), F32)
    for j in range(4):
        picked += jnp.where(quarter == j, 1.0, 0.0) * gsum[0:1, j * L : (j + 1) * L]
    o_gg[...] = picked

    for i, tt in enumerate((t1, t2, t3)):
        g_copy(i, tt).wait_send()
    for m in range(MB):
        for k in range(2):
            hid_copy(m, k, 0).wait_send()
            hid_copy(m, k, 1).wait_send()

            @pl.when(s == 0)
            def _():
                hid_copy(m, k, 2).wait_send()

            @pl.when(s < SECTIONS - 1)
            def _():
                l_copy(m, k).wait_send()

            for i in range(2):
                m_copy(m, i, k).wait_send()
            b_copy(m, k).wait_send()

            @pl.when(s > 0)
            def _():
                a_copy(m, k).wait_send()

        for layer in range(SECTIONS - 1):
            @pl.when((s < SECTIONS - 1) & (s >= layer))
            def _():
                p_copy(m, pown.at[m], layer, t, 0).wait_send()
                p_copy(m, pown.at[m], layer, t, 1).wait_send()

            @pl.when(s > layer)
            def _():
                p_copy(m, pown.at[m], layer, t, 2).wait_send()
                p_copy(m, pown.at[m], layer, t2, 3).wait_send()

        for rz in range(8):
            u_copy(m, rz).wait_send()
            if rz:
                u_pass_copy(m, rz).wait_send()
        q_drain(m)
    for i in range(2):
        x_copy(i).wait_send()
    for block in range(2):
        for j in range(4):
            @pl.when(jnp.logical_not(loop & (lax.rem(d, 8) == 4 * block + j)))
            def _():
                gg_copy(block, j).wait_send()


def hand_out(*refs):
    for i in range(4):
        refs[4 + i][...] = refs[i][...]


def body(hidden_in, teacher, segment_ids, w_query, w_keyval, norm_gain):
    vmem = pl.BlockSpec(memory_space=pltpu.VMEM)
    hbm = pl.BlockSpec(memory_space=pl.ANY)
    dma = pltpu.SemaphoreType.DMA
    V = pltpu.VMEM
    out = pl.pallas_call(
        kernel,
        out_shape=(
            jax.ShapeDtypeStruct((1, ROWS, QC), F32),
            jax.ShapeDtypeStruct((1, ROWS, KC), F32),
            jax.ShapeDtypeStruct((1, L), F32),
            jax.ShapeDtypeStruct((1, 1, MB, L, BLK), BF),
        ),
        in_specs=[vmem, vmem, vmem, hbm, hbm, vmem],
        out_specs=(vmem, vmem, vmem, vmem),
        scratch_shapes=[
            V((D, C), BF),
            V((MB, TENSOR, 2, L, HB), BF),
            V((DP, 8, ROWS), F32),
            V((L, C), F32),
            V((MB, L, C), BF),
            V((MB, 2, 4 * L, L), F32),
            V((MB, L, L), F32),
            V((MB, L, 128), F32),
            V((MB, 3, L, HD), BF),
            V((MB, SECTIONS - 1, TENSOR, 3, L, HD), BF),
            V((MB, 2, L, HB), BF),
            V((MB, 8, 5, L, HD), BF),
            V((MB, DP, 5, L, HD), BF),
            V((MB, 2, 2 * L, HD), BF),
            V((MB, DP, 2 * L, HD), BF),
            V((2, L, HD), BF),
            V((2, 2 * HD, HB), BF),
            V((MB, L, C), BF),
            V((MB, DP, L, HB + HD), BF),
            V((MB, 2, 2, L, HB), BF),
            V((MB, 2, 2, L, HB), BF),
            V((MB, 2, L, HB), BF),
            V((MB, 2, L, HB), BF),
            V((MB, 2, L, HB), BF),
            V((MB, 2, L, HB), BF),
            V((MB, 2, L, HB), BF),
            V((MB, 2, L, HB), BF),
            V((2, 2, HD, HB + HD), F32),
            V((2, HD, HB + HD), BF),
            V((2, HD, HB + HD), BF),
            V((2, 8, ROWS), F32),
            V((8, 8, ROWS), F32),
            dma((2, TENSOR)),
            dma((3,)),
            dma((TENSOR,)),
            dma((MB, 3, 2)),
            dma((MB, TENSOR, 2)),
            dma((MB, SECTIONS - 1, 4)),
            dma((MB, SECTIONS - 1, TENSOR)),
            dma((MB, DP)),
            dma((MB, DP)),
            dma((MB, DP)),
            dma((MB, DP)),
            dma((MB, 2, 2)),
            dma((MB, 2, 2)),
            dma((2, MB, 2)),
            dma((MB, 2)),
            dma((MB, 2)),
            dma((MB, 2)),
            dma((MB, 2)),
            dma((MB, 2)),
            dma((8,)),
            dma((8,)),
            dma((2,)),
            dma((2,)),
        ],
        compiler_params=pltpu.CompilerParams(
            collective_id=1, has_side_effects=True, vmem_limit_bytes=58 * 1024 * 1024
        ),
        name="train_step",
    )(hidden_in, teacher, segment_ids, w_query, w_keyval, norm_gain)
    return pl.pallas_call(
        hand_out,
        out_shape=tuple(jax.ShapeDtypeStruct(o.shape, o.dtype) for o in out),
        in_specs=[vmem] * 4,
        out_specs=(vmem,) * 4,
        name="hand_out",
    )(*out)


def solution(mesh):
    in_specs = (
        P("dp", None, None, "tensor"),
        P("dp", None, None, "tensor"),
        P("dp", None, None),
        P("section", None, "tensor"),
        P("section", None, "tensor"),
        P("section", "tensor"),
    )
    out_specs = (
        P("section", "dp", "tensor"),
        P("section", "dp", "tensor"),
        P("section", ("tensor", "dp")),
        P("section", "dp", None, None, "tensor"),
    )
    return jax.shard_map(body, mesh=mesh, in_specs=in_specs, out_specs=out_specs, check_vma=False)
```

```python
import math

import jax
import jax.numpy as jnp
from jax import lax
from jax.experimental import pallas as pl
from jax.experimental.pallas import tpu as pltpu
from jax.sharding import PartitionSpec as P

EPSILON = 1e-05
D = 4096
HD = 128
L = 64
W = 32
MB = 2
DP = 16
SECTIONS = 4
TENSOR = 4
ROWS = D // DP
QC = 1024
KC = 256
C = QC + KC
BLK = 1024
HB = BLK // 2
BF = jnp.bfloat16
F32 = jnp.float32
MESH = pl.DeviceIdType.MESH
SCALE = 1.0 / math.sqrt(HD)
NT = (((1,), (1,)), ((), ()))
TN = (((0,), (0,)), ((), ()))
NN = (((1,), (0,)), ((), ()))


def dot(a, b, dims=NN):
    return lax.dot_general(a, b, dims, preferred_element_type=F32)


def place(rz, c):
    rz = rz % 8
    near = 0 if rz == 0 else 2 * rz - 1 if rz <= 4 else 2 * (8 - rz)
    return 2 * near + c


def stack_heads(x):
    return jnp.concatenate([x[:, i * HD : (i + 1) * HD] for i in range(x.shape[1] // HD)], axis=0)


def unstack_heads(x):
    return jnp.concatenate([x[i * L : (i + 1) * L] for i in range(x.shape[0] // L)], axis=1)


def kernel(
    hid, tea, seg, wq, wkv, gain,
    o_gq, o_gkv, o_gg, o_lig,
    w, hidv, teav, hbuf, g16, acc, qkv, probs, mask, invb, pown, pbuf, dyb,
    usend, uall, qown, qs, low, kdiag, dqkv, dqall, msend, mrecv, bsend, asend, abuf, bbuf, bfin, lig, gtot, xsend, xrecv, ggsend, ggrecv,
    w_sem, in_sem, g_ssem, g_rsem, h_ssem, h_rsem, p_ssem, p_rsem, u_ssem, u_rsem, q_ssem, q_rsem,
    m_ssem, m_rsem, ab_ssem, a_rsem, b_rsem, f_rsem, l_ssem, l_rsem, gg_ssem, gg_rsem, x_ssem, x_rsem,
):
    s = lax.axis_index("section")
    d = lax.axis_index("dp")
    t = lax.axis_index("tensor")
    t1 = t + 1 - 2 * lax.rem(t, 2)
    t2 = lax.rem(t + 2, 4)
    t3 = 3 - t
    z = d // 2
    xl = lax.rem(d, 2)
    sn = lax.rem(s + 1, SECTIONS)
    sp = lax.rem(s + SECTIONS - 1, SECTIONS)

    def rcopy(src, dst, ssem, rsem, dev):
        return pltpu.make_async_remote_copy(
            src_ref=src, dst_ref=dst, send_sem=ssem, recv_sem=rsem, device_id=dev, device_id_type=MESH
        )

    bar = pltpu.get_barrier_semaphore()
    for dev in ((s, d, t1), (s, d, t2), (s, d, t3), (sn, d, t), (sn, d, t2), (sp, d, t), (sp, d, t2)):
        pl.semaphore_signal(bar, inc=1, device_id=dev, device_id_type=MESH)

    def greet(i, _):
        pl.semaphore_signal(bar, inc=1, device_id=(s, lax.rem(d + i, DP), t), device_id_type=MESH)
        return 0

    lax.fori_loop(1, DP, greet, 0)
    loop = (t == z // 2) & (z // 4 == lax.rem(z, 2))
    zs = 2 * t + d // 8
    for i in range(8):
        @pl.when(jnp.logical_not(loop & (t == i // 2) & (xl == i % 2)))
        def _():
            pl.semaphore_signal(bar, inc=1, device_id=(s, 2 * zs + i % 2, i // 2), device_id_type=MESH)

    def w_copies(j):
        rows = pl.ds(pl.multiple_of(j * BLK, BLK), BLK)
        return (
            pltpu.make_async_copy(wq.at[0, rows, :], w.at[rows, pl.ds(0, QC)], w_sem.at[0, j]),
            pltpu.make_async_copy(wkv.at[0, rows, :], w.at[rows, pl.ds(QC, KC)], w_sem.at[1, j]),
        )

    def in_copy(i, m, k):
        src = (hid, tea)[i].at[0, m, :, pl.ds(k * HB, HB)]
        return pltpu.make_async_copy(src, (hidv, teav)[i].at[m, k], in_sem.at[i, m, k])

    for i in range(2):
        for m in range(MB):
            for k in range(2):
                in_copy(i, m, k).start()
    for j in (t, t2, t1, t3):
        for c in w_copies(j):
            c.start()

    ri = lax.broadcasted_iota(jnp.int32, (L, L), 0)
    ci = lax.broadcasted_iota(jnp.int32, (L, L), 1)
    for m in range(MB):
        srow = jnp.broadcast_to(seg[0, m : m + 1, :], (L, L))
        scol = jnp.sum(jnp.where(ri == ci, srow, 0), axis=1, keepdims=True)
        mask[m] = jnp.where((srow == scol) & (ri >= ci), 1.0, 0.0)
    fi = lax.broadcasted_iota(jnp.int32, (L, HD), 0)
    fj = lax.rem(lax.broadcasted_iota(jnp.int32, (L, HD), 1), W)
    low[0] = jnp.where(fj > fi - W, 1.0, 0.0).astype(BF)
    low[1] = jnp.where(fj > fi - W, 0.0, 1.0).astype(BF)
    kdiag[...] = jnp.zeros_like(kdiag)
    for i in range(4):
        g16[4 * t + i] = jnp.broadcast_to(gain[:, i * ROWS : (i + 1) * ROWS].astype(F32), (8, ROWS))

    for m in range(MB):
        for k in range(2):
            in_copy(0, m, k).wait()
    pl.semaphore_wait(bar, 30 - jnp.where(loop, 1, 0))

    def g_copy(i, dev_t):
        sl = g16.at[pl.ds(4 * t, 4)]
        return rcopy(sl, sl, g_ssem.at[i], g_rsem.at[t], (s, d, dev_t))

    def hid_copy(m, k, kind):
        slot = t2 if kind == 2 else t
        src = hbuf.at[m, slot, k] if kind == 2 else hidv.at[m, k]
        return rcopy(
            src, hbuf.at[m, slot, k], h_ssem.at[m, kind, k], h_rsem.at[m, slot, k], (s, d, t1 if kind else t2)
        )

    def h_wait(m, slot, k):
        blk = hbuf.at[m, slot, k]
        rcopy(blk, blk, h_ssem.at[m, 0, k], h_rsem.at[m, slot, k], (s, d, t1)).wait_recv()

    def p_copy(m, src, layer, slot, kind):
        dev = ((sn, d, t), (sn, d, t2), (s, d, t1), (s, d, t1))[kind]
        return rcopy(
            src, pbuf.at[m, layer, slot], p_ssem.at[m, layer, kind], p_rsem.at[m, layer, slot], dev
        )

    def p_wait(m, layer, slot):
        p_copy(m, pbuf.at[m, layer, slot], layer, slot, 2).wait_recv()

    for i, tt in enumerate((t1, t2, t3)):
        g_copy(i, tt).start()

    for m in range(MB):
        for k in range(2):
            hid_copy(m, k, 0).start()
            hid_copy(m, k, 1).start()
            hbuf[m, t, k] = hidv[m, k]
            in_copy(1, m, k).wait()

    for tt in (t1, t2, t3):
        sl = g16.at[pl.ds(4 * tt, 4)]
        rcopy(sl, sl, g_ssem.at[0], g_rsem.at[tt], (s, d, tt)).wait_recv()

    def gains(j, k):
        p = 4 * j + 2 * k
        return jnp.concatenate([g16[p, 0:1, :], g16[p + 1, 0:1, :]], axis=1)

    def forward(m):
        ss = jnp.zeros((L, 1), F32)

        def kstep(j, first):
            x0 = hbuf[m, j, 0].astype(F32)
            x1 = hbuf[m, j, 1].astype(F32)
            xg = jnp.concatenate([(x0 * gains(j, 0)).astype(BF), (x1 * gains(j, 1)).astype(BF)], axis=1)
            part = dot(xg, w[pl.ds(pl.multiple_of(j * BLK, BLK), BLK), :])
            if first:
                acc[...] = part
            else:
                acc[...] += part
            return jnp.sum(x0 * x0 + x1 * x1, axis=1, keepdims=True)

        def need_w(j):
            if m == 0:
                for c in w_copies(j):
                    c.wait()

        def rebuild(layer, j, b):
            vd = kdiag.at[b]
            for h in range(4):
                vd[h * W : (h + 1) * W, h * HD : (h + 1) * HD] = pbuf[m, layer, j, 2, :W]
                vd[HD + h * W : HD + (h + 1) * W, h * HD : (h + 1) * HD] = pbuf[m, layer, j, 2, W:]
            for k in range(2):
                fold = pbuf[m, layer, j, k]
                both = jnp.concatenate([fold * low[0], fold * low[1]], axis=1)
                o = dot(both, vd[...]).astype(BF)
                hbuf[m, j, k] = (hbuf[m, j, k].astype(F32) + o.astype(F32)).astype(BF)

        for k in range(2):
            h_wait(m, t2, k)
            hid_copy(m, k, 2).start()

        @pl.when(s > 0)
        def _():
            for k in range(2):
                hid_copy(m, k, 2).wait_send()

        for layer in range(SECTIONS - 1):
            @pl.when(s > layer)
            def _():
                mine = pbuf.at[m, layer, t]
                p_wait(m, layer, t)
                p_copy(m, mine, layer, t, 2).start()

                @pl.when(s < SECTIONS - 1)
                def _():
                    p_copy(m, mine, layer, t, 1).start()
                    p_copy(m, mine, layer, t, 0).start()

                p_wait(m, layer, t2)
                p_copy(m, pbuf.at[m, layer, t2], layer, t2, 3).start()
                rebuild(layer, t, 0)
                rebuild(layer, t2, 1)

        need_w(t)
        ss += kstep(t, True)
        need_w(t2)
        ss += kstep(t2, False)
        for j in (t1, t3):
            for k in range(2):
                h_wait(m, j, k)
        for layer in range(SECTIONS - 1):
            @pl.when(s > layer)
            def _():
                p_wait(m, layer, t1)
                rebuild(layer, t1, 0)
                p_wait(m, layer, t3)
                rebuild(layer, t3, 1)

        for j in (t1, t3):
            need_w(j)
            ss += kstep(j, False)
        inv = lax.rsqrt(ss / D + EPSILON)
        invb[m] = jnp.broadcast_to(inv, (L, 128))
        qkv[m] = (acc[...] * inv).astype(BF)
        key = qkv[m, :, QC : QC + HD]
        val = qkv[m, :, QC + HD :]
        allowed = jnp.concatenate([mask[m]] * 4, axis=0) > 0.0
        for k in range(2):
            q = stack_heads(qkv[m, :, k * HB : (k + 1) * HB])
            sc = dot(q, key, NT) * SCALE
            e = jnp.exp(jnp.where(allowed, sc, -1e30))
            pr = e / jnp.sum(e, axis=1, keepdims=True)
            probs[m, k] = pr
            fold = (pr[:, :W] + pr[:, W:]).astype(BF)
            for h in range(4):
                pown[m, k, :, h * W : (h + 1) * W] = fold[h * L : (h + 1) * L]

            @pl.when(s == SECTIONS - 1)
            def _():
                o = unstack_heads(dot(pr.astype(BF), val).astype(BF)).astype(F32)
                hn = (hbuf[m, t, k].astype(F32) + o).astype(BF)
                dyb[m, k] = (
                    hn.astype(F32) - teav[m, k].astype(F32)
                ).astype(BF)

        pown[m, 2] = val

        @pl.when(s < SECTIONS - 1)
        def _():
            p_copy(m, pown.at[m], s, t, 1).start()
            p_copy(m, pown.at[m], s, t, 0).start()

    def peer(rz, c):
        return (s, 2 * lax.rem(z + rz % 8, 8) + (1 - xl if c else xl), t)

    def u_copy(m, rz):
        slot = place(-rz, 0) if rz else place(0, 1)
        src = usend.at[m, lax.rem(z + rz, 8) if rz else z]
        return rcopy(src, uall.at[m, slot], u_ssem.at[m, slot], u_rsem.at[m, slot], peer(rz, 0 if rz else 1))

    def u_pass_copy(m, rz):
        slot = place(rz, 1)
        return rcopy(
            uall.at[m, place(rz, 0)], uall.at[m, slot], u_ssem.at[m, slot], u_rsem.at[m, slot], peer(0, 1)
        )

    def u_pass(m):
        for rz in (1, 7, 2, 6, 3, 5, 4):
            u_wait_one(m, place(rz, 0))
            u_pass_copy(m, rz).start()

    def u_wait_one(m, i):
        blk = uall.at[m, i]
        rcopy(blk, blk, u_ssem.at[m, i], u_rsem.at[m, i], peer(1, 0)).wait_recv()

    def send_rows(m):
        inv = invb[m, :, 0:1]
        for j in range(TENSOR):
            for k in range(2):
                u = (hbuf[m, j, k].astype(F32) * inv).astype(BF)
                for i in range(4):
                    usend[m, 2 * j + k, i] = u[:, i * HD : (i + 1) * HD]
        for p in range(8):
            usend[m, p, 4] = qkv[m, :, QC : QC + HD]
        uall[m, 0] = usend[m, z]
        for rz in (0, 1, 7, 2, 6, 3, 5, 4):
            u_copy(m, rz).start()


    def q_copy(m, src, rz, c, step, dc):
        dst = place(rz - step, c ^ dc)
        return rcopy(src, qs.at[m, dst], q_ssem.at[m, dst], q_rsem.at[m, dst], peer(step, dc))

    def q_wait(m, rz, c):
        blk = qs.at[m, place(rz, c)]
        rcopy(blk, blk, q_ssem.at[m, 0], q_rsem.at[m, place(rz, c)], peer(1, 0)).wait_recv()

    def q_start(m):
        qs[m, 0] = qown[m, xl]
        for step in (2, 6, 1, 7, 0):
            for c in range(2):
                if step or c:
                    q_copy(m, qown.at[m, 1 - xl if c else xl], 0, 0, step, c).start()

    def q_hop(m):
        for c in range(2):
            for sg in (1, -1):
                q_wait(m, -2 * sg, c)
                src = qs.at[m, place(-2 * sg, c)]
                q_copy(m, src, -2 * sg, c, sg, 0).start()
                if c == (0 if sg == 1 else 1):
                    q_copy(m, src, -2 * sg, c, 2 * sg, 0).start()

    def q_near(m):
        for rz, c in ((0, 1), (1, 0), (-1, 0), (1, 1), (-1, 1)):
            q_wait(m, rz, c)

    def q_far(m):
        for rz in (3, -3, 4):
            for c in range(2):
                q_wait(m, rz, c)

    def q_make(m, lo, hi):
        for i in range(lo, hi):
            pair = kdiag.at[i % 2]
            for h in range(4):
                pair[h * W : (h + 1) * W, h * HD : (h + 1) * HD] = uall[m, i, 4, :W]
                pair[HD + h * W : HD + (h + 1) * W, h * HD : (h + 1) * HD] = uall[m, i, 4, W:]
            fold = qs[m, i, :L, :]
            both = jnp.concatenate([fold * low[0], fold * low[1]], axis=1)
            dqall[m, i, :, :HB] = (dot(both, pair[...]) * SCALE).astype(BF)
            dqall[m, i, :, HB:] = qs[m, i, L:, :]

    def q_drain(m):
        for i in range(1, DP):
            blk = qs.at[m, i]
            rcopy(blk, blk, q_ssem.at[m, i], q_rsem.at[m, i], peer(1, 0)).wait_send()

    def m_copy(m, i, k):
        return rcopy(msend.at[m, i, k], mrecv.at[m, i, k], m_ssem.at[m, i, k], m_rsem.at[m, i, k], (s, d, t1))

    def a_copy(m, k):
        return rcopy(asend.at[m, k], abuf.at[m, k], ab_ssem.at[0, m, k], a_rsem.at[m, k], (sp, d, t))

    def b_copy(m, k):
        return rcopy(bsend.at[m, k], bbuf.at[m, k], ab_ssem.at[1, m, k], b_rsem.at[m, k], (sp, d, t2))

    def f_copy(m, k):
        return rcopy(bsend.at[m, k], bfin.at[m, k], ab_ssem.at[1, m, k], f_rsem.at[m, k], (s, d, t2))

    def l_copy(m, k):
        return rcopy(dyb.at[m, k], lig.at[m, k], l_ssem.at[m, k], l_rsem.at[m, k], (sn, d, t))

    def early_hop():
        @pl.when(s == 0)
        def _():
            q_hop(0)

    def backward(m):
        key = qkv[m, :, QC : QC + HD]
        val = qkv[m, :, QC + HD :]
        inv = invb[m, :, 0:1]
        dk = jnp.zeros((L, HD), F32)
        dv = jnp.zeros((L, HD), F32)
        rd = jnp.zeros((L, 1), F32)
        for k in range(2):
            @pl.when(s < SECTIONS - 1)
            def _():
                a_copy(m, k).wait_recv()
                b_copy(m, k).wait_recv()
                dyb[m, k] = (abuf[m, k].astype(F32) + bbuf[m, k].astype(F32)).astype(BF)
                l_copy(m, k).start()

            do = stack_heads(dyb[m, k])
            q = stack_heads(qkv[m, :, k * HB : (k + 1) * HB])
            pr = probs[m, k]
            dp = dot(do, val, NT)
            ds = pr * (dp - jnp.sum(dp * pr, axis=1, keepdims=True))
            dsb = ds.astype(BF)
            dq = (dot(dsb, key) * SCALE).astype(BF)
            dqkv[m, :, k * HB : (k + 1) * HB] = unstack_heads(dq)
            fold = (ds[:, :W] + ds[:, W:]).astype(BF)
            for h in range(4):
                qown[m, k, :L, h * W : (h + 1) * W] = fold[h * L : (h + 1) * L]
            dk += dot(dsb, q, TN)
            dv += dot(pr.astype(BF), do, TN)
            qd = jnp.sum(q.astype(F32) * dq.astype(F32), axis=1, keepdims=True)
            for i in range(4):
                rd += qd[i * L : (i + 1) * L]
        dkb = (dk * SCALE).astype(BF)
        dvb = dv.astype(BF)
        dqkv[m, :, QC : QC + HD] = dkb
        dqkv[m, :, QC + HD :] = dvb
        qown[m, 0, L:, :] = dkb
        qown[m, 1, L:, :] = dvb
        rd += jnp.sum(
            key.astype(F32) * dkb.astype(F32) + val.astype(F32) * dvb.astype(F32), axis=1, keepdims=True
        )
        q_start(m)
        if m == 1:
            early_hop()
        coef = inv * inv * rd / D
        grads = dqkv[m]

        def term(j, k):
            part = dot(grads, w[pl.ds(pl.multiple_of(j * BLK + k * HB, HB), HB), :], NT)
            return inv * gains(j, k) * part - hbuf[m, j, k].astype(F32) * coef

        for k in range(2):
            for i, j in enumerate((t3, t1)):
                msend[m, i, k] = term(j, k).astype(BF)
                m_copy(m, i, k).start()
        for k in range(2):
            own = term(t2, k)
            m_copy(m, 0, k).wait_recv()
            bsend[m, k] = (own + mrecv[m, 0, k].astype(F32)).astype(BF)

            @pl.when(s > 0)
            def _():
                b_copy(m, k).start()

            @pl.when(s == 0)
            def _():
                f_copy(m, k).start()

            own = term(t, k) + dyb[m, k].astype(F32)
            m_copy(m, 1, k).wait_recv()
            asend[m, k] = (own + mrecv[m, 1, k].astype(F32)).astype(BF)

            @pl.when(s > 0)
            def _():
                a_copy(m, k).start()

    forward(0)

    @pl.when(s == SECTIONS - 1)
    def _():
        backward(0)
        send_rows(0)

    forward(1)

    @pl.when(s < SECTIONS - 1)
    def _():
        for m in range(MB):
            send_rows(m)

    @pl.when(s < 2)
    def _():
        for m in range(MB):
            u_pass(m)

    @pl.when(s < SECTIONS - 1)
    def _():
        backward(0)

    backward(1)

    @pl.when(s == SECTIONS - 1)
    def _():
        send_rows(1)

    @pl.when(s > 0)
    def _():
        q_hop(0)

    @pl.when(s >= 2)
    def _():
        for m in range(MB):
            u_pass(m)

    def u_wait(m):
        for rz in range(8):
            u_wait_one(m, place(rz, 1))

    def weight_grads(m, lo, hi, block, i):
        u = uall[m, lo:hi, 2 * block + i].reshape((hi - lo) * L, HD)
        g = dqall[m, lo:hi].reshape((hi - lo) * L, HB + HD)
        part = dot(u, g, TN)
        if m == 0 and lo == 0:
            gtot[block, i] = part
        else:
            gtot[block, i] += part

    u_wait(0)
    q_near(0)
    q_make(0, 0, 10)
    q_hop(1)
    u_wait(1)
    q_far(0)
    q_make(0, 10, DP)
    q_near(1)
    q_make(1, 0, 10)
    for block in range(2):
        for i in range(2):
            weight_grads(0, 0, DP, block, i)
            weight_grads(1, 0, 10, block, i)

    @pl.when(s == 0)
    def _():
        for m in range(MB):
            for k in range(2):
                f_copy(m, k).wait_recv()
                lig[m, k] = (asend[m, k].astype(F32) + bfin[m, k].astype(F32)).astype(BF)

    @pl.when(s > 0)
    def _():
        for m in range(MB):
            for k in range(2):
                l_copy(m, k).wait_recv()

    for m in range(MB):
        for k in range(2):
            o_lig[0, 0, m, :, k * HB : (k + 1) * HB] = lig[m, k]

    q_far(1)
    q_make(1, 10, DP)

    def x_copy(i):
        return rcopy(xsend.at[i], xrecv.at[i], x_ssem.at[i], x_rsem.at[i], peer(0, 1))

    for i in range(2):
        weight_grads(1, 10, DP, 1 - xl, i)
        xsend[i] = gtot[1 - xl, i].astype(BF)
        x_copy(i).start()
    for i in range(2):
        weight_grads(1, 10, DP, xl, i)

    eye = lax.broadcasted_iota(jnp.int32, (HD, HD), 0) == lax.broadcasted_iota(jnp.int32, (HD, HD), 1)
    for block in range(2):
        for i in range(2):
            rows = pl.ds(pl.multiple_of((2 * z + block) * ROWS + i * HD, HD), HD)
            wide = w[rows, pl.ds(pl.multiple_of(xl * HB, HB), HB)].astype(F32)
            narrow = w[rows, pl.ds(pl.multiple_of(QC + xl * HD, HD), HD)].astype(F32)
            total = gtot[block, i]
            col = jnp.sum(total[:, :HB] * wide, axis=1, keepdims=True) + jnp.sum(
                total[:, HB:] * narrow, axis=1, keepdims=True
            )
            row = jnp.sum(jnp.where(eye, jnp.broadcast_to(col, (HD, HD)), 0.0), axis=0, keepdims=True)
            ggsend[block, :, i * HD : (i + 1) * HD] = jnp.broadcast_to(row, (8, HD))

    def gg_copy(block, j):
        n = 4 * block + j
        src = 2 * t + xl
        return rcopy(
            ggsend.at[block], ggrecv.at[src], gg_ssem.at[n], gg_rsem.at[src], (s, 8 * lax.rem(z, 2) + n, z // 2)
        )

    for block in range(2):
        for j in range(4):
            mine = loop & (lax.rem(d, 8) == 4 * block + j)

            @pl.when(jnp.logical_not(mine))
            def _():
                gg_copy(block, j).start()

            @pl.when(mine)
            def _():
                ggrecv[2 * t + xl] = ggsend[block]

    for i in range(2):
        x_copy(i).wait_recv()
        grow = g16[d, 0:1, i * HD : (i + 1) * HD]
        gcol = jnp.sum(jnp.where(eye, jnp.broadcast_to(grow, (HD, HD)), 0.0), axis=1, keepdims=True)
        own = gtot[xl, i]
        other = xrecv[i].astype(F32)
        first = jnp.where(xl == 0, own, other) * gcol
        second = jnp.where(xl == 0, other, own) * gcol
        rs = slice(i * HD, (i + 1) * HD)
        o_gq[0, rs, :HB] = first[:, :HB]
        o_gq[0, rs, HB:] = second[:, :HB]
        o_gkv[0, rs, :HD] = first[:, HB:]
        o_gkv[0, rs, HD:] = second[:, HB:]

    gsum = jnp.zeros((8, ROWS), F32)
    for i in range(8):
        @pl.when(jnp.logical_not(loop & (t == i // 2) & (xl == i % 2)))
        def _():
            rcopy(
                ggsend.at[0], ggrecv.at[i], gg_ssem.at[0], gg_rsem.at[i], (s, 2 * zs + i % 2, i // 2)
            ).wait_recv()
        gsum += ggrecv[i]
    quarter = lax.rem(d, 4)
    picked = jnp.zeros((1, L), F32)
    for j in range(4):
        picked += jnp.where(quarter == j, 1.0, 0.0) * gsum[0:1, j * L : (j + 1) * L]
    o_gg[...] = picked

    for i, tt in enumerate((t1, t2, t3)):
        g_copy(i, tt).wait_send()
    for m in range(MB):
        for k in range(2):
            hid_copy(m, k, 0).wait_send()
            hid_copy(m, k, 1).wait_send()

            @pl.when(s == 0)
            def _():
                hid_copy(m, k, 2).wait_send()

            @pl.when(s < SECTIONS - 1)
            def _():
                l_copy(m, k).wait_send()

            for i in range(2):
                m_copy(m, i, k).wait_send()
            b_copy(m, k).wait_send()

            @pl.when(s > 0)
            def _():
                a_copy(m, k).wait_send()

        for layer in range(SECTIONS - 1):
            @pl.when((s < SECTIONS - 1) & (s >= layer))
            def _():
                p_copy(m, pown.at[m], layer, t, 0).wait_send()
                p_copy(m, pown.at[m], layer, t, 1).wait_send()

            @pl.when(s > layer)
            def _():
                p_copy(m, pown.at[m], layer, t, 2).wait_send()
                p_copy(m, pown.at[m], layer, t2, 3).wait_send()

        for rz in range(8):
            u_copy(m, rz).wait_send()
            if rz:
                u_pass_copy(m, rz).wait_send()
        q_drain(m)
    for i in range(2):
        x_copy(i).wait_send()
    for block in range(2):
        for j in range(4):
            @pl.when(jnp.logical_not(loop & (lax.rem(d, 8) == 4 * block + j)))
            def _():
                gg_copy(block, j).wait_send()


def hand_out(*refs):
    src, dst, held = refs[:4], refs[4:8], refs[8:12]
    isem, osem = refs[12:]
    parts = [(0, slice(i * L, (i + 1) * L)) for i in range(4)] + [(1, None), (3, None), (2, None)]

    def at(ref, part):
        return ref if part is None else ref.at[:, part]

    ins = [pltpu.make_async_copy(at(src[i], q), at(held[i], q), isem.at[n]) for n, (i, q) in enumerate(parts)]
    outs = [pltpu.make_async_copy(at(held[i], q), at(dst[i], q), osem.at[n]) for n, (i, q) in enumerate(parts)]
    for c in ins:
        c.start()
    for i, o in zip(ins, outs):
        i.wait()
        o.start()
    for o in outs:
        o.wait()


def body(hidden_in, teacher, segment_ids, w_query, w_keyval, norm_gain):
    vmem = pl.BlockSpec(memory_space=pltpu.VMEM)
    hbm = pl.BlockSpec(memory_space=pl.ANY)
    dma = pltpu.SemaphoreType.DMA
    V = pltpu.VMEM
    out = pl.pallas_call(
        kernel,
        out_shape=(
            jax.ShapeDtypeStruct((1, ROWS, QC), F32),
            jax.ShapeDtypeStruct((1, ROWS, KC), F32),
            jax.ShapeDtypeStruct((1, L), F32),
            jax.ShapeDtypeStruct((1, 1, MB, L, BLK), BF),
        ),
        in_specs=[hbm, hbm, vmem, hbm, hbm, vmem],
        out_specs=(vmem, vmem, vmem, vmem),
        scratch_shapes=[
            V((D, C), BF),
            V((MB, 2, L, HB), BF),
            V((MB, 2, L, HB), BF),
            V((MB, TENSOR, 2, L, HB), BF),
            V((DP, 8, ROWS), F32),
            V((L, C), F32),
            V((MB, L, C), BF),
            V((MB, 2, 4 * L, L), F32),
            V((MB, L, L), F32),
            V((MB, L, 128), F32),
            V((MB, 3, L, HD), BF),
            V((MB, SECTIONS - 1, TENSOR, 3, L, HD), BF),
            V((MB, 2, L, HB), BF),
            V((MB, 8, 5, L, HD), BF),
            V((MB, DP, 5, L, HD), BF),
            V((MB, 2, 2 * L, HD), BF),
            V((MB, DP, 2 * L, HD), BF),
            V((2, L, HD), BF),
            V((2, 2 * HD, HB), BF),
            V((MB, L, C), BF),
            V((MB, DP, L, HB + HD), BF),
            V((MB, 2, 2, L, HB), BF),
            V((MB, 2, 2, L, HB), BF),
            V((MB, 2, L, HB), BF),
            V((MB, 2, L, HB), BF),
            V((MB, 2, L, HB), BF),
            V((MB, 2, L, HB), BF),
            V((MB, 2, L, HB), BF),
            V((MB, 2, L, HB), BF),
            V((2, 2, HD, HB + HD), F32),
            V((2, HD, HB + HD), BF),
            V((2, HD, HB + HD), BF),
            V((2, 8, ROWS), F32),
            V((8, 8, ROWS), F32),
            dma((2, TENSOR)),
            dma((2, MB, 2)),
            dma((3,)),
            dma((TENSOR,)),
            dma((MB, 3, 2)),
            dma((MB, TENSOR, 2)),
            dma((MB, SECTIONS - 1, 4)),
            dma((MB, SECTIONS - 1, TENSOR)),
            dma((MB, DP)),
            dma((MB, DP)),
            dma((MB, DP)),
            dma((MB, DP)),
            dma((MB, 2, 2)),
            dma((MB, 2, 2)),
            dma((2, MB, 2)),
            dma((MB, 2)),
            dma((MB, 2)),
            dma((MB, 2)),
            dma((MB, 2)),
            dma((MB, 2)),
            dma((8,)),
            dma((8,)),
            dma((2,)),
            dma((2,)),
        ],
        compiler_params=pltpu.CompilerParams(
            collective_id=1, has_side_effects=True, vmem_limit_bytes=58 * 1024 * 1024
        ),
        name="train_step",
    )(hidden_in, teacher, segment_ids, w_query, w_keyval, norm_gain)
    return pl.pallas_call(
        hand_out,
        out_shape=tuple(jax.ShapeDtypeStruct(o.shape, o.dtype) for o in out),
        in_specs=[hbm] * 4,
        out_specs=(hbm,) * 4,
        scratch_shapes=[V(o.shape, o.dtype) for o in out] + [dma((7,)), dma((7,))],
        name="hand_out",
    )(*out)


def solution(mesh):
    in_specs = (
        P("dp", None, None, "tensor"),
        P("dp", None, None, "tensor"),
        P("dp", None, None),
        P("section", None, "tensor"),
        P("section", None, "tensor"),
        P("section", "tensor"),
    )
    out_specs = (
        P("section", "dp", "tensor"),
        P("section", "dp", "tensor"),
        P("section", ("tensor", "dp")),
        P("section", "dp", None, None, "tensor"),
    )
    return jax.shard_map(body, mesh=mesh, in_specs=in_specs, out_specs=out_specs, check_vma=False)
```

```python
import math

import jax
import jax.numpy as jnp
from jax import lax
from jax.experimental import pallas as pl
from jax.experimental.pallas import tpu as pltpu
from jax.sharding import PartitionSpec as P

EPSILON = 1e-05
D = 4096
HD = 128
L = 64
W = 32
MB = 2
DP = 16
SECTIONS = 4
TENSOR = 4
ROWS = D // DP
QC = 1024
KC = 256
C = QC + KC
BLK = 1024
HB = BLK // 2
BF = jnp.bfloat16
F32 = jnp.float32
MESH = pl.DeviceIdType.MESH
SCALE = 1.0 / math.sqrt(HD)
NT = (((1,), (1,)), ((), ()))
TN = (((0,), (0,)), ((), ()))
NN = (((1,), (0,)), ((), ()))


def dot(a, b, dims=NN):
    return lax.dot_general(a, b, dims, preferred_element_type=F32)


def place(rz, c):
    rz = rz % 8
    near = 0 if rz == 0 else 2 * rz - 1 if rz <= 4 else 2 * (8 - rz)
    return 2 * near + c


def stack_heads(x):
    return jnp.concatenate([x[:, i * HD : (i + 1) * HD] for i in range(x.shape[1] // HD)], axis=0)


def unstack_heads(x):
    return jnp.concatenate([x[i * L : (i + 1) * L] for i in range(x.shape[0] // L)], axis=1)


def kernel(
    hid, tea, seg, wq, wkv, gain,
    o_gq, o_gkv, o_gg, o_lig,
    w, hidv, teav, hbuf, g16, acc, qkv, probs, mask, invb, pown, pbuf, dyb,
    usend, uall, qown, qs, low, kdiag, dqkv, dqall, msend, mrecv, bsend, asend, abuf, bbuf, bfin, lig, gtot, xsend, xrecv, ggsend, ggrecv,
    w_sem, in_sem, g_ssem, g_rsem, h_ssem, h_rsem, p_ssem, p_rsem, u_ssem, u_rsem, q_ssem, q_rsem,
    m_ssem, m_rsem, ab_ssem, a_rsem, b_rsem, f_rsem, l_ssem, l_rsem, gg_ssem, gg_rsem, x_ssem, x_rsem,
):
    s = lax.axis_index("section")
    d = lax.axis_index("dp")
    t = lax.axis_index("tensor")
    t1 = t + 1 - 2 * lax.rem(t, 2)
    t2 = lax.rem(t + 2, 4)
    t3 = 3 - t
    z = d // 2
    xl = lax.rem(d, 2)
    sn = lax.rem(s + 1, SECTIONS)
    sp = lax.rem(s + SECTIONS - 1, SECTIONS)

    def rcopy(src, dst, ssem, rsem, dev):
        return pltpu.make_async_remote_copy(
            src_ref=src, dst_ref=dst, send_sem=ssem, recv_sem=rsem, device_id=dev, device_id_type=MESH
        )

    bar = pltpu.get_barrier_semaphore()
    for dev in ((s, d, t1), (s, d, t2), (s, d, t3), (sn, d, t), (sn, d, t2), (sp, d, t), (sp, d, t2)):
        pl.semaphore_signal(bar, inc=1, device_id=dev, device_id_type=MESH)

    def greet(i, _):
        pl.semaphore_signal(bar, inc=1, device_id=(s, lax.rem(d + i, DP), t), device_id_type=MESH)
        return 0

    lax.fori_loop(1, DP, greet, 0)
    loop = (t == z // 2) & (z // 4 == lax.rem(z, 2))
    zs = 2 * t + d // 8
    for i in range(8):
        @pl.when(jnp.logical_not(loop & (t == i // 2) & (xl == i % 2)))
        def _():
            pl.semaphore_signal(bar, inc=1, device_id=(s, 2 * zs + i % 2, i // 2), device_id_type=MESH)

    def w_copies(j):
        rows = pl.ds(pl.multiple_of(j * BLK, BLK), BLK)
        return (
            pltpu.make_async_copy(wq.at[0, rows, :], w.at[rows, pl.ds(0, QC)], w_sem.at[0, j]),
            pltpu.make_async_copy(wkv.at[0, rows, :], w.at[rows, pl.ds(QC, KC)], w_sem.at[1, j]),
        )

    def in_copy(i, m, k):
        src = (hid, tea)[i].at[0, m, :, pl.ds(k * HB, HB)]
        return pltpu.make_async_copy(src, (hidv, teav)[i].at[m, k], in_sem.at[i, m, k])

    for i in range(2):
        for m in range(MB):
            for k in range(2):
                in_copy(i, m, k).start()
    for j in (t, t2, t1, t3):
        for c in w_copies(j):
            c.start()

    ri = lax.broadcasted_iota(jnp.int32, (L, L), 0)
    ci = lax.broadcasted_iota(jnp.int32, (L, L), 1)
    for m in range(MB):
        srow = jnp.broadcast_to(seg[0, m : m + 1, :], (L, L))
        scol = jnp.sum(jnp.where(ri == ci, srow, 0), axis=1, keepdims=True)
        mask[m] = jnp.where((srow == scol) & (ri >= ci), 1.0, 0.0)
    fi = lax.broadcasted_iota(jnp.int32, (L, HD), 0)
    fj = lax.rem(lax.broadcasted_iota(jnp.int32, (L, HD), 1), W)
    low[0] = jnp.where(fj > fi - W, 1.0, 0.0).astype(BF)
    low[1] = jnp.where(fj > fi - W, 0.0, 1.0).astype(BF)
    kdiag[...] = jnp.zeros_like(kdiag)
    for i in range(4):
        g16[4 * t + i] = jnp.broadcast_to(gain[:, i * ROWS : (i + 1) * ROWS].astype(F32), (8, ROWS))

    for m in range(MB):
        for k in range(2):
            in_copy(0, m, k).wait()
    pl.semaphore_wait(bar, 30 - jnp.where(loop, 1, 0))

    def g_copy(i, dev_t):
        sl = g16.at[pl.ds(4 * t, 4)]
        return rcopy(sl, sl, g_ssem.at[i], g_rsem.at[t], (s, d, dev_t))

    def hid_copy(m, k, kind):
        slot = t2 if kind == 2 else t
        src = hbuf.at[m, slot, k] if kind == 2 else hidv.at[m, k]
        return rcopy(
            src, hbuf.at[m, slot, k], h_ssem.at[m, kind, k], h_rsem.at[m, slot, k], (s, d, t1 if kind else t2)
        )

    def h_wait(m, slot, k):
        blk = hbuf.at[m, slot, k]
        rcopy(blk, blk, h_ssem.at[m, 0, k], h_rsem.at[m, slot, k], (s, d, t1)).wait_recv()

    def p_copy(m, src, layer, slot, kind):
        dev = ((sn, d, t), (sn, d, t2), (s, d, t1), (s, d, t1))[kind]
        return rcopy(
            src, pbuf.at[m, layer, slot], p_ssem.at[m, layer, kind], p_rsem.at[m, layer, slot], dev
        )

    def p_wait(m, layer, slot):
        p_copy(m, pbuf.at[m, layer, slot], layer, slot, 2).wait_recv()

    for i, tt in enumerate((t1, t2, t3)):
        g_copy(i, tt).start()

    for m in range(MB):
        for k in range(2):
            hid_copy(m, k, 0).start()
            hid_copy(m, k, 1).start()
            hbuf[m, t, k] = hidv[m, k]
            in_copy(1, m, k).wait()

    for tt in (t1, t2, t3):
        sl = g16.at[pl.ds(4 * tt, 4)]
        rcopy(sl, sl, g_ssem.at[0], g_rsem.at[tt], (s, d, tt)).wait_recv()

    def gains(j, k):
        p = 4 * j + 2 * k
        return jnp.concatenate([g16[p, 0:1, :], g16[p + 1, 0:1, :]], axis=1)

    def forward(m):
        ss = jnp.zeros((L, 1), F32)

        def kstep(j, first):
            x0 = hbuf[m, j, 0].astype(F32)
            x1 = hbuf[m, j, 1].astype(F32)
            xg = jnp.concatenate([(x0 * gains(j, 0)).astype(BF), (x1 * gains(j, 1)).astype(BF)], axis=1)
            part = dot(xg, w[pl.ds(pl.multiple_of(j * BLK, BLK), BLK), :])
            if first:
                acc[...] = part
            else:
                acc[...] += part
            return jnp.sum(x0 * x0 + x1 * x1, axis=1, keepdims=True)

        def need_w(j):
            if m == 0:
                for c in w_copies(j):
                    c.wait()

        def rebuild(layer, j, b):
            vd = kdiag.at[b]
            for h in range(4):
                vd[h * W : (h + 1) * W, h * HD : (h + 1) * HD] = pbuf[m, layer, j, 2, :W]
                vd[HD + h * W : HD + (h + 1) * W, h * HD : (h + 1) * HD] = pbuf[m, layer, j, 2, W:]
            for k in range(2):
                fold = pbuf[m, layer, j, k]
                both = jnp.concatenate([fold * low[0], fold * low[1]], axis=1)
                o = dot(both, vd[...]).astype(BF)
                hbuf[m, j, k] = (hbuf[m, j, k].astype(F32) + o.astype(F32)).astype(BF)

        for k in range(2):
            h_wait(m, t2, k)
            hid_copy(m, k, 2).start()

        @pl.when(s > 0)
        def _():
            for k in range(2):
                hid_copy(m, k, 2).wait_send()

        for layer in range(SECTIONS - 1):
            @pl.when(s > layer)
            def _():
                mine = pbuf.at[m, layer, t]
                p_wait(m, layer, t)
                p_copy(m, mine, layer, t, 2).start()

                @pl.when(s < SECTIONS - 1)
                def _():
                    p_copy(m, mine, layer, t, 1).start()
                    p_copy(m, mine, layer, t, 0).start()

                p_wait(m, layer, t2)
                p_copy(m, pbuf.at[m, layer, t2], layer, t2, 3).start()
                rebuild(layer, t, 0)
                rebuild(layer, t2, 1)

        need_w(t)
        ss += kstep(t, True)
        need_w(t2)
        ss += kstep(t2, False)
        for j in (t1, t3):
            for k in range(2):
                h_wait(m, j, k)
        for layer in range(SECTIONS - 1):
            @pl.when(s > layer)
            def _():
                p_wait(m, layer, t1)
                rebuild(layer, t1, 0)
                p_wait(m, layer, t3)
                rebuild(layer, t3, 1)

        for j in (t1, t3):
            need_w(j)
            ss += kstep(j, False)
        inv = lax.rsqrt(ss / D + EPSILON)
        invb[m] = jnp.broadcast_to(inv, (L, 128))
        qkv[m] = (acc[...] * inv).astype(BF)
        key = qkv[m, :, QC : QC + HD]
        val = qkv[m, :, QC + HD :]
        allowed = jnp.concatenate([mask[m]] * 4, axis=0) > 0.0
        for k in range(2):
            q = stack_heads(qkv[m, :, k * HB : (k + 1) * HB])
            sc = dot(q, key, NT) * SCALE
            e = jnp.exp(jnp.where(allowed, sc, -1e30))
            pr = e / jnp.sum(e, axis=1, keepdims=True)
            probs[m, k] = pr
            fold = (pr[:, :W] + pr[:, W:]).astype(BF)
            for h in range(4):
                pown[m, k, :, h * W : (h + 1) * W] = fold[h * L : (h + 1) * L]

            @pl.when(s == SECTIONS - 1)
            def _():
                o = unstack_heads(dot(pr.astype(BF), val).astype(BF)).astype(F32)
                hn = (hbuf[m, t, k].astype(F32) + o).astype(BF)
                dyb[m, k] = (
                    hn.astype(F32) - teav[m, k].astype(F32)
                ).astype(BF)

        pown[m, 2] = val

        @pl.when(s < SECTIONS - 1)
        def _():
            p_copy(m, pown.at[m], s, t, 1).start()
            p_copy(m, pown.at[m], s, t, 0).start()

    def peer(rz, c):
        return (s, 2 * lax.rem(z + rz % 8, 8) + (1 - xl if c else xl), t)

    def u_copy(m, rz):
        slot = place(-rz, 0) if rz else place(0, 1)
        src = usend.at[m, lax.rem(z + rz, 8) if rz else z]
        return rcopy(src, uall.at[m, slot], u_ssem.at[m, slot], u_rsem.at[m, slot], peer(rz, 0 if rz else 1))

    def u_pass_copy(m, rz):
        slot = place(rz, 1)
        return rcopy(
            uall.at[m, place(rz, 0)], uall.at[m, slot], u_ssem.at[m, slot], u_rsem.at[m, slot], peer(0, 1)
        )

    def u_pass(m):
        for rz in (1, 7, 2, 6, 3, 5, 4):
            u_wait_one(m, place(rz, 0))
            u_pass_copy(m, rz).start()

    def u_wait_one(m, i):
        blk = uall.at[m, i]
        rcopy(blk, blk, u_ssem.at[m, i], u_rsem.at[m, i], peer(1, 0)).wait_recv()

    def send_rows(m):
        inv = invb[m, :, 0:1]
        for j in range(TENSOR):
            for k in range(2):
                u = (hbuf[m, j, k].astype(F32) * inv).astype(BF)
                for i in range(4):
                    usend[m, 2 * j + k, i] = u[:, i * HD : (i + 1) * HD]
        for p in range(8):
            usend[m, p, 4] = qkv[m, :, QC : QC + HD]
        uall[m, 0] = usend[m, z]
        for rz in (0, 1, 7, 2, 6, 3, 5, 4):
            u_copy(m, rz).start()


    def q_copy(m, src, rz, c, step, dc):
        dst = place(rz - step, c ^ dc)
        return rcopy(src, qs.at[m, dst], q_ssem.at[m, dst], q_rsem.at[m, dst], peer(step, dc))

    def q_wait(m, rz, c):
        blk = qs.at[m, place(rz, c)]
        rcopy(blk, blk, q_ssem.at[m, 0], q_rsem.at[m, place(rz, c)], peer(1, 0)).wait_recv()

    def q_start(m):
        qs[m, 0] = qown[m, xl]
        for step in (2, 6, 1, 7, 0):
            for c in range(2):
                if step or c:
                    q_copy(m, qown.at[m, 1 - xl if c else xl], 0, 0, step, c).start()

    def q_hop(m):
        for c in range(2):
            for sg in (1, -1):
                q_wait(m, -2 * sg, c)
                src = qs.at[m, place(-2 * sg, c)]
                q_copy(m, src, -2 * sg, c, sg, 0).start()
                if c == (0 if sg == 1 else 1):
                    q_copy(m, src, -2 * sg, c, 2 * sg, 0).start()

    def q_near(m):
        for rz, c in ((0, 1), (1, 0), (-1, 0), (1, 1), (-1, 1)):
            q_wait(m, rz, c)

    def q_far(m):
        for rz in (3, -3, 4):
            for c in range(2):
                q_wait(m, rz, c)

    def q_make(m, lo, hi):
        for i in range(lo, hi):
            pair = kdiag.at[i % 2]
            for h in range(4):
                pair[h * W : (h + 1) * W, h * HD : (h + 1) * HD] = uall[m, i, 4, :W]
                pair[HD + h * W : HD + (h + 1) * W, h * HD : (h + 1) * HD] = uall[m, i, 4, W:]
            fold = qs[m, i, :L, :]
            both = jnp.concatenate([fold * low[0], fold * low[1]], axis=1)
            dqall[m, i, :, :HB] = (dot(both, pair[...]) * SCALE).astype(BF)
            dqall[m, i, :, HB:] = qs[m, i, L:, :]

    def q_drain(m):
        for i in range(1, DP):
            blk = qs.at[m, i]
            rcopy(blk, blk, q_ssem.at[m, i], q_rsem.at[m, i], peer(1, 0)).wait_send()

    def m_copy(m, i, k):
        return rcopy(msend.at[m, i, k], mrecv.at[m, i, k], m_ssem.at[m, i, k], m_rsem.at[m, i, k], (s, d, t1))

    def a_copy(m, k):
        return rcopy(asend.at[m, k], abuf.at[m, k], ab_ssem.at[0, m, k], a_rsem.at[m, k], (sp, d, t))

    def b_copy(m, k):
        return rcopy(bsend.at[m, k], bbuf.at[m, k], ab_ssem.at[1, m, k], b_rsem.at[m, k], (sp, d, t2))

    def f_copy(m, k):
        return rcopy(bsend.at[m, k], bfin.at[m, k], ab_ssem.at[1, m, k], f_rsem.at[m, k], (s, d, t2))

    def l_copy(m, k):
        return rcopy(dyb.at[m, k], lig.at[m, k], l_ssem.at[m, k], l_rsem.at[m, k], (sn, d, t))

    def early_hop():
        @pl.when(s == 0)
        def _():
            q_hop(0)

    def backward(m):
        key = qkv[m, :, QC : QC + HD]
        val = qkv[m, :, QC + HD :]
        inv = invb[m, :, 0:1]
        dk = jnp.zeros((L, HD), F32)
        dv = jnp.zeros((L, HD), F32)
        rd = jnp.zeros((L, 1), F32)
        for k in range(2):
            @pl.when(s < SECTIONS - 1)
            def _():
                a_copy(m, k).wait_recv()
                b_copy(m, k).wait_recv()
                dyb[m, k] = (abuf[m, k].astype(F32) + bbuf[m, k].astype(F32)).astype(BF)
                l_copy(m, k).start()

            do = stack_heads(dyb[m, k])
            q = stack_heads(qkv[m, :, k * HB : (k + 1) * HB])
            pr = probs[m, k]
            dp = dot(do, val, NT)
            ds = pr * (dp - jnp.sum(dp * pr, axis=1, keepdims=True))
            dsb = ds.astype(BF)
            dq = (dot(dsb, key) * SCALE).astype(BF)
            dqkv[m, :, k * HB : (k + 1) * HB] = unstack_heads(dq)
            fold = (ds[:, :W] + ds[:, W:]).astype(BF)
            for h in range(4):
                qown[m, k, :L, h * W : (h + 1) * W] = fold[h * L : (h + 1) * L]
            dk += dot(dsb, q, TN)
            dv += dot(pr.astype(BF), do, TN)
            qd = jnp.sum(q.astype(F32) * dq.astype(F32), axis=1, keepdims=True)
            for i in range(4):
                rd += qd[i * L : (i + 1) * L]
        dkb = (dk * SCALE).astype(BF)
        dvb = dv.astype(BF)
        dqkv[m, :, QC : QC + HD] = dkb
        dqkv[m, :, QC + HD :] = dvb
        qown[m, 0, L:, :] = dkb
        qown[m, 1, L:, :] = dvb
        rd += jnp.sum(
            key.astype(F32) * dkb.astype(F32) + val.astype(F32) * dvb.astype(F32), axis=1, keepdims=True
        )
        q_start(m)
        if m == 1:
            early_hop()
        coef = inv * inv * rd / D
        grads = dqkv[m]

        def term(j, k):
            part = dot(grads, w[pl.ds(pl.multiple_of(j * BLK + k * HB, HB), HB), :], NT)
            return inv * gains(j, k) * part - hbuf[m, j, k].astype(F32) * coef

        for k in range(2):
            for i, j in enumerate((t3, t1)):
                msend[m, i, k] = term(j, k).astype(BF)
                m_copy(m, i, k).start()
        for k in range(2):
            own = term(t2, k)
            m_copy(m, 0, k).wait_recv()
            bsend[m, k] = (own + mrecv[m, 0, k].astype(F32)).astype(BF)

            @pl.when(s > 0)
            def _():
                b_copy(m, k).start()

            @pl.when(s == 0)
            def _():
                f_copy(m, k).start()

            own = term(t, k) + dyb[m, k].astype(F32)
            m_copy(m, 1, k).wait_recv()
            asend[m, k] = (own + mrecv[m, 1, k].astype(F32)).astype(BF)

            @pl.when(s > 0)
            def _():
                a_copy(m, k).start()

    forward(0)

    @pl.when(s == SECTIONS - 1)
    def _():
        backward(0)
        send_rows(0)

    forward(1)

    @pl.when(s < SECTIONS - 1)
    def _():
        for m in range(MB):
            send_rows(m)

    @pl.when(s < 2)
    def _():
        for m in range(MB):
            u_pass(m)

    @pl.when(s < SECTIONS - 1)
    def _():
        backward(0)

    @pl.when(s == 2)
    def _():
        u_pass(0)

    backward(1)

    @pl.when(s == SECTIONS - 1)
    def _():
        send_rows(1)

    @pl.when(s > 0)
    def _():
        q_hop(0)

    @pl.when(s == 3)
    def _():
        u_pass(0)

    @pl.when(s >= 2)
    def _():
        u_pass(1)

    def u_wait(m):
        for rz in range(8):
            u_wait_one(m, place(rz, 1))

    def weight_grads(m, lo, hi, block, i):
        u = uall[m, lo:hi, 2 * block + i].reshape((hi - lo) * L, HD)
        g = dqall[m, lo:hi].reshape((hi - lo) * L, HB + HD)
        part = dot(u, g, TN)
        if m == 0 and lo == 0:
            gtot[block, i] = part
        else:
            gtot[block, i] += part

    u_wait(0)
    q_near(0)
    q_make(0, 0, 10)
    q_hop(1)
    u_wait(1)
    q_far(0)
    q_make(0, 10, DP)
    q_near(1)
    q_make(1, 0, 10)
    for block in range(2):
        for i in range(2):
            weight_grads(0, 0, DP, block, i)
            weight_grads(1, 0, 10, block, i)

    @pl.when(s == 0)
    def _():
        for m in range(MB):
            for k in range(2):
                f_copy(m, k).wait_recv()
                lig[m, k] = (asend[m, k].astype(F32) + bfin[m, k].astype(F32)).astype(BF)

    @pl.when(s > 0)
    def _():
        for m in range(MB):
            for k in range(2):
                l_copy(m, k).wait_recv()

    for m in range(MB):
        for k in range(2):
            o_lig[0, 0, m, :, k * HB : (k + 1) * HB] = lig[m, k]

    q_far(1)
    q_make(1, 10, DP)

    def x_copy(i):
        return rcopy(xsend.at[i], xrecv.at[i], x_ssem.at[i], x_rsem.at[i], peer(0, 1))

    for i in range(2):
        weight_grads(1, 10, DP, 1 - xl, i)
        xsend[i] = gtot[1 - xl, i].astype(BF)
        x_copy(i).start()
    for i in range(2):
        weight_grads(1, 10, DP, xl, i)

    eye = lax.broadcasted_iota(jnp.int32, (HD, HD), 0) == lax.broadcasted_iota(jnp.int32, (HD, HD), 1)
    for block in range(2):
        for i in range(2):
            rows = pl.ds(pl.multiple_of((2 * z + block) * ROWS + i * HD, HD), HD)
            wide = w[rows, pl.ds(pl.multiple_of(xl * HB, HB), HB)].astype(F32)
            narrow = w[rows, pl.ds(pl.multiple_of(QC + xl * HD, HD), HD)].astype(F32)
            total = gtot[block, i]
            col = jnp.sum(total[:, :HB] * wide, axis=1, keepdims=True) + jnp.sum(
                total[:, HB:] * narrow, axis=1, keepdims=True
            )
            row = jnp.sum(jnp.where(eye, jnp.broadcast_to(col, (HD, HD)), 0.0), axis=0, keepdims=True)
            ggsend[block, :, i * HD : (i + 1) * HD] = jnp.broadcast_to(row, (8, HD))

    def gg_copy(block, j):
        n = 4 * block + j
        src = 2 * t + xl
        return rcopy(
            ggsend.at[block], ggrecv.at[src], gg_ssem.at[n], gg_rsem.at[src], (s, 8 * lax.rem(z, 2) + n, z // 2)
        )

    for block in range(2):
        for j in range(4):
            mine = loop & (lax.rem(d, 8) == 4 * block + j)

            @pl.when(jnp.logical_not(mine))
            def _():
                gg_copy(block, j).start()

            @pl.when(mine)
            def _():
                ggrecv[2 * t + xl] = ggsend[block]

    for i in range(2):
        x_copy(i).wait_recv()
        grow = g16[d, 0:1, i * HD : (i + 1) * HD]
        gcol = jnp.sum(jnp.where(eye, jnp.broadcast_to(grow, (HD, HD)), 0.0), axis=1, keepdims=True)
        own = gtot[xl, i]
        other = xrecv[i].astype(F32)
        first = jnp.where(xl == 0, own, other) * gcol
        second = jnp.where(xl == 0, other, own) * gcol
        rs = slice(i * HD, (i + 1) * HD)
        o_gq[0, rs, :HB] = first[:, :HB]
        o_gq[0, rs, HB:] = second[:, :HB]
        o_gkv[0, rs, :HD] = first[:, HB:]
        o_gkv[0, rs, HD:] = second[:, HB:]

    gsum = jnp.zeros((8, ROWS), F32)
    for i in range(8):
        @pl.when(jnp.logical_not(loop & (t == i // 2) & (xl == i % 2)))
        def _():
            rcopy(
                ggsend.at[0], ggrecv.at[i], gg_ssem.at[0], gg_rsem.at[i], (s, 2 * zs + i % 2, i // 2)
            ).wait_recv()
        gsum += ggrecv[i]
    quarter = lax.rem(d, 4)
    picked = jnp.zeros((1, L), F32)
    for j in range(4):
        picked += jnp.where(quarter == j, 1.0, 0.0) * gsum[0:1, j * L : (j + 1) * L]
    o_gg[...] = picked

    for i, tt in enumerate((t1, t2, t3)):
        g_copy(i, tt).wait_send()
    for m in range(MB):
        for k in range(2):
            hid_copy(m, k, 0).wait_send()
            hid_copy(m, k, 1).wait_send()

            @pl.when(s == 0)
            def _():
                hid_copy(m, k, 2).wait_send()

            @pl.when(s < SECTIONS - 1)
            def _():
                l_copy(m, k).wait_send()

            for i in range(2):
                m_copy(m, i, k).wait_send()
            b_copy(m, k).wait_send()

            @pl.when(s > 0)
            def _():
                a_copy(m, k).wait_send()

        for layer in range(SECTIONS - 1):
            @pl.when((s < SECTIONS - 1) & (s >= layer))
            def _():
                p_copy(m, pown.at[m], layer, t, 0).wait_send()
                p_copy(m, pown.at[m], layer, t, 1).wait_send()

            @pl.when(s > layer)
            def _():
                p_copy(m, pown.at[m], layer, t, 2).wait_send()
                p_copy(m, pown.at[m], layer, t2, 3).wait_send()

        for rz in range(8):
            u_copy(m, rz).wait_send()
            if rz:
                u_pass_copy(m, rz).wait_send()
        q_drain(m)
    for i in range(2):
        x_copy(i).wait_send()
    for block in range(2):
        for j in range(4):
            @pl.when(jnp.logical_not(loop & (lax.rem(d, 8) == 4 * block + j)))
            def _():
                gg_copy(block, j).wait_send()


def hand_out(*refs):
    src, dst, held = refs[:4], refs[4:8], refs[8:12]
    isem, osem = refs[12:]
    parts = [(0, slice(i * L, (i + 1) * L)) for i in range(4)] + [(1, None), (3, None), (2, None)]

    def at(ref, part):
        return ref if part is None else ref.at[:, part]

    ins = [pltpu.make_async_copy(at(src[i], q), at(held[i], q), isem.at[n]) for n, (i, q) in enumerate(parts)]
    outs = [pltpu.make_async_copy(at(held[i], q), at(dst[i], q), osem.at[n]) for n, (i, q) in enumerate(parts)]
    for c in ins:
        c.start()
    for i, o in zip(ins, outs):
        i.wait()
        o.start()
    for o in outs:
        o.wait()


def body(hidden_in, teacher, segment_ids, w_query, w_keyval, norm_gain):
    vmem = pl.BlockSpec(memory_space=pltpu.VMEM)
    hbm = pl.BlockSpec(memory_space=pl.ANY)
    dma = pltpu.SemaphoreType.DMA
    V = pltpu.VMEM
    out = pl.pallas_call(
        kernel,
        out_shape=(
            jax.ShapeDtypeStruct((1, ROWS, QC), F32),
            jax.ShapeDtypeStruct((1, ROWS, KC), F32),
            jax.ShapeDtypeStruct((1, L), F32),
            jax.ShapeDtypeStruct((1, 1, MB, L, BLK), BF),
        ),
        in_specs=[hbm, hbm, vmem, hbm, hbm, vmem],
        out_specs=(vmem, vmem, vmem, vmem),
        scratch_shapes=[
            V((D, C), BF),
            V((MB, 2, L, HB), BF),
            V((MB, 2, L, HB), BF),
            V((MB, TENSOR, 2, L, HB), BF),
            V((DP, 8, ROWS), F32),
            V((L, C), F32),
            V((MB, L, C), BF),
            V((MB, 2, 4 * L, L), F32),
            V((MB, L, L), F32),
            V((MB, L, 128), F32),
            V((MB, 3, L, HD), BF),
            V((MB, SECTIONS - 1, TENSOR, 3, L, HD), BF),
            V((MB, 2, L, HB), BF),
            V((MB, 8, 5, L, HD), BF),
            V((MB, DP, 5, L, HD), BF),
            V((MB, 2, 2 * L, HD), BF),
            V((MB, DP, 2 * L, HD), BF),
            V((2, L, HD), BF),
            V((2, 2 * HD, HB), BF),
            V((MB, L, C), BF),
            V((MB, DP, L, HB + HD), BF),
            V((MB, 2, 2, L, HB), BF),
            V((MB, 2, 2, L, HB), BF),
            V((MB, 2, L, HB), BF),
            V((MB, 2, L, HB), BF),
            V((MB, 2, L, HB), BF),
            V((MB, 2, L, HB), BF),
            V((MB, 2, L, HB), BF),
            V((MB, 2, L, HB), BF),
            V((2, 2, HD, HB + HD), F32),
            V((2, HD, HB + HD), BF),
            V((2, HD, HB + HD), BF),
            V((2, 8, ROWS), F32),
            V((8, 8, ROWS), F32),
            dma((2, TENSOR)),
            dma((2, MB, 2)),
            dma((3,)),
            dma((TENSOR,)),
            dma((MB, 3, 2)),
            dma((MB, TENSOR, 2)),
            dma((MB, SECTIONS - 1, 4)),
            dma((MB, SECTIONS - 1, TENSOR)),
            dma((MB, DP)),
            dma((MB, DP)),
            dma((MB, DP)),
            dma((MB, DP)),
            dma((MB, 2, 2)),
            dma((MB, 2, 2)),
            dma((2, MB, 2)),
            dma((MB, 2)),
            dma((MB, 2)),
            dma((MB, 2)),
            dma((MB, 2)),
            dma((MB, 2)),
            dma((8,)),
            dma((8,)),
            dma((2,)),
            dma((2,)),
        ],
        compiler_params=pltpu.CompilerParams(
            collective_id=1, has_side_effects=True, vmem_limit_bytes=58 * 1024 * 1024
        ),
        name="train_step",
    )(hidden_in, teacher, segment_ids, w_query, w_keyval, norm_gain)
    return pl.pallas_call(
        hand_out,
        out_shape=tuple(jax.ShapeDtypeStruct(o.shape, o.dtype) for o in out),
        in_specs=[hbm] * 4,
        out_specs=(hbm,) * 4,
        scratch_shapes=[V(o.shape, o.dtype) for o in out] + [dma((7,)), dma((7,))],
        name="hand_out",
    )(*out)


def solution(mesh):
    in_specs = (
        P("dp", None, None, "tensor"),
        P("dp", None, None, "tensor"),
        P("dp", None, None),
        P("section", None, "tensor"),
        P("section", None, "tensor"),
        P("section", "tensor"),
    )
    out_specs = (
        P("section", "dp", "tensor"),
        P("section", "dp", "tensor"),
        P("section", ("tensor", "dp")),
        P("section", "dp", None, None, "tensor"),
    )
    return jax.shard_map(body, mesh=mesh, in_specs=in_specs, out_specs=out_specs, check_vma=False)
```
